32 devices in a mesh: leaf: 8 (over z, x), front: 4 (over y, core).
Axes of the slice: x: 2, y: 2, z: 4, core: 2. Of those that a mesh axis runs over, the one named last changes fastest.
Arguments:
- leaf_update: float32 [4096, 512], P('leaf', 'front'), as said below
- front_entries1: float32 [4096, 1024], P('leaf', 'front'), as said below
- front_entries2: float32 [2048, 1024], replicated, as said below
- front_entries3: float32 [1024, 1024], replicated, as said below
- map_leaf: int32 [8, 4], replicated, may hold values from 0 to 7, all different within a row
- map_mid: int32 [4, 4], replicated, may hold values from 0 to 7, all different within a row
- map_top: int32 [2, 4], replicated, may hold values from 0 to 7, as said below
Outputs:
- leaf_inverse: float32 [4096, 512], P('leaf', 'front')
The draws below stay inside these ranges and needn't reach their ends.
Inputs may be any that keep to these rules, and one draw needn't show every extreme that they name: `map_leaf`: row s gives, for each block of 128 rows of subtree s's update, the block of its first level front that receives it; the entries of a row are distinct. `map_mid`: row k gives, for each block of 128 rows of the update of first level node k, the block of second level front k // 2 that receives it; the entries of a row are distinct. `map_top`: row n gives, for each block of 128 rows of the update of second level node n, the block of the top front that receives it; the entries of a row are distinct, and every block of the top front is named by at least one of the two rows. `leaf_update`: each block of 512 rows is symmetric and positive definite. `front_entries1`: each front's block is symmetric and positive definite. `front_entries2`: each front's block is symmetric and positive definite. `front_entries3`: symmetric and positive definite.
All inputs are finite; a program needn't handle non-finite values.
Results may differ from the reference program's by a relative error of at most 0.00017.
Values sent between devices are 32-bit elements; how exact they have to be, the bound alone decides.
No kernel may reach another device: no remote copies, remote signals or barrier semaphores. Data moves between devices by JAX's collectives and lax.ppermute only.
A program may use at most 128 MiB of HBM per device.

```python
import jax
import jax.numpy as jnp
from jax import lax

BLK = 128
R0 = 512
SEP1 = 512
SEP2 = 512
SEP3 = 1024
RUP = 512
SUBTREES = 8
N_LEAF = 8


def spd_blocks(key, count, order, weight, lowest, highest):
    first_key, second_key = jax.random.split(key, 2)
    samples = jax.random.normal(first_key, (count, order, order), jnp.float32)
    gram = jnp.einsum('cik,cjk->cij', samples, samples, precision=lax.Precision.HIGHEST) / order
    gram = 0.5 * (gram + jnp.swapaxes(gram, 1, 2))
    diagonal = jax.random.uniform(second_key, (count, order), jnp.float32, lowest, highest)
    matrix = weight * (gram + diagonal[:, :, None] * jnp.eye(order, dtype=jnp.float32)[None])
    return matrix.reshape(count * order, order)


def draw_leaf_update(key, part):
    return spd_blocks(jax.random.fold_in(key, 11), SUBTREES, R0, 0.1, 0.05, 0.15)


def draw_front_entries1(key, part):
    return spd_blocks(jax.random.fold_in(key, 12), 4, SEP1 + RUP, 1.0, 0.03, 0.09)


def draw_front_entries2(key, part):
    return spd_blocks(jax.random.fold_in(key, 13), 2, SEP2 + RUP, 1.0, 0.03, 0.09)


def draw_front_entries3(key, part):
    return spd_blocks(jax.random.fold_in(key, 14), 1, SEP3, 1.0, 0.03, 0.09)


def draw_map_top(key, part):
    top_blocks = SEP3 // BLK
    child_blocks = RUP // BLK
    shuffled = jax.random.permutation(jax.random.fold_in(key, 15), jnp.arange(top_blocks, dtype=jnp.int32))
    first_row = shuffled[:child_blocks]
    second_row = shuffled[top_blocks - child_blocks:]
    return jnp.stack([first_row, second_row], axis=0).astype(jnp.int32)


def picks_of(own_key, rows, count, top, lift):
    order = jax.random.permutation(jax.random.fold_in(own_key, 1), count)
    pull = order
    for power in range(3):
        pull = pull * pull // count
    pull = pull * lift // count
    lots = jax.random.randint(jax.random.fold_in(own_key, 2), (rows, count), 0, 4096) + pull
    sure = jax.random.permutation(jax.random.fold_in(own_key, 3), rows)[jnp.arange(count) % rows]
    lots = jnp.where(jnp.arange(rows)[:, None] == sure[None, :], 1 << 14, lots)
    merit = lots * count + jnp.arange(count)
    return lax.top_k(merit.astype(jnp.int32), top)[1].astype(jnp.int32)


def setup_inputs(seed: int = 0) -> dict:
    key_list = jax.random.split(jax.random.key(seed), 8)
    return {
        "leaf_update": draw_leaf_update(jax.random.fold_in(key_list[7], 71), 0),
        "front_entries1": draw_front_entries1(jax.random.fold_in(key_list[7], 71), 0),
        "front_entries2": draw_front_entries2(jax.random.fold_in(key_list[7], 71), 0),
        "front_entries3": draw_front_entries3(jax.random.fold_in(key_list[7], 71), 0),
        "map_leaf": picks_of(key_list[4], SUBTREES, (SEP1 + RUP) // BLK, R0 // BLK, 0),
        "map_mid": picks_of(key_list[5], 4, (SEP2 + RUP) // BLK, RUP // BLK, 0),
        "map_top": draw_map_top(jax.random.fold_in(key_list[7], 71), 0),
    }


def product(left_side, right_side):
    return jnp.dot(left_side, right_side, precision=lax.Precision.HIGHEST)

def selector(block_list, parent_blocks):
    return (block_list[:, None] == jnp.arange(parent_blocks, dtype=jnp.int32)[None, :]).astype(jnp.float32)

def extend(update, picker):
    child_blocks, parent_blocks = picker.shape
    block_rows = update.shape[0] // child_blocks
    blocked = update.reshape(child_blocks, block_rows, child_blocks, block_rows)
    result = jnp.einsum('ia,jb,ixjy->axby', picker, picker, blocked, precision=lax.Precision.HIGHEST)
    return result.reshape(parent_blocks * block_rows, parent_blocks * block_rows)

def extract(sigma, picker):
    child_blocks, parent_blocks = picker.shape
    block_rows = sigma.shape[0] // parent_blocks
    blocked = sigma.reshape(parent_blocks, block_rows, parent_blocks, block_rows)
    result = jnp.einsum('ia,jb,axby->ixjy', picker, picker, blocked, precision=lax.Precision.HIGHEST)
    return result.reshape(child_blocks * block_rows, child_blocks * block_rows)

def expand(picker, block_rows):
    child_blocks, parent_blocks = picker.shape
    identity = jnp.eye(block_rows, dtype=jnp.float32)
    result = jnp.einsum('ia,xy->axiy', picker, identity, precision=lax.Precision.HIGHEST)
    return result.reshape(parent_blocks * block_rows, child_blocks * block_rows)

def factor(assembled, separator):
    factor_ss = jnp.linalg.cholesky(assembled[:separator, :separator])
    solved = lax.linalg.triangular_solve(factor_ss, assembled[:separator, separator:], left_side=True, lower=True)
    factor_rs = solved.T
    update = assembled[separator:, separator:] - product(factor_rs, solved)
    return (factor_ss, factor_rs, update)

def inverse(factor_ss, factor_rs, sigma_rr):
    separator = factor_ss.shape[0]
    identity = jnp.eye(separator, dtype=jnp.float32)
    inverse_ss = lax.linalg.triangular_solve(factor_ss, identity, left_side=True, lower=True)
    coupling = product(factor_rs, inverse_ss)
    sigma_rs = -product(sigma_rr, coupling)
    sigma_ss = product(inverse_ss.T, inverse_ss) - product(coupling.T, sigma_rs)
    upper_rows = jnp.concatenate([sigma_ss, sigma_rs.T], axis=1)
    lower_rows = jnp.concatenate([sigma_rs, sigma_rr], axis=1)
    return jnp.concatenate([upper_rows, lower_rows], axis=0)

def reference(leaf_update, front_entries1, front_entries2, front_entries3, map_leaf, map_mid, map_top):
    members = N_LEAF // 4
    order_one = SEP1 + RUP
    order_two = SEP2 + RUP
    first_level = []
    for node_index in range(4):
        assembled = front_entries1[node_index * order_one:(node_index + 1) * order_one]
        for subtree in range(node_index * members, (node_index + 1) * members):
            piece = leaf_update[subtree * R0:(subtree + 1) * R0]
            assembled = assembled + extend(piece, selector(map_leaf[subtree], order_one // BLK))
        first_level.append(factor(assembled, SEP1))
    second_level = []
    for node_index in range(2):
        assembled = front_entries2[node_index * order_two:(node_index + 1) * order_two]
        assembled = assembled + extend(first_level[2 * node_index][2], selector(map_mid[2 * node_index], order_two // BLK))
        assembled = assembled + extend(first_level[2 * node_index + 1][2], selector(map_mid[2 * node_index + 1], order_two // BLK))
        second_level.append(factor(assembled, SEP2))
    assembled = front_entries3 + extend(second_level[0][2], selector(map_top[0], SEP3 // BLK))
    assembled = assembled + extend(second_level[1][2], selector(map_top[1], SEP3 // BLK))
    factor_top = jnp.linalg.cholesky(assembled)
    sigma_second = []
    for node_index in range(2):
        basis = expand(selector(map_top[node_index], SEP3 // BLK), BLK)
        solved = lax.linalg.triangular_solve(factor_top, basis, left_side=True, lower=True)
        sigma_rr = product(solved.T, solved)
        sigma_second.append(inverse(second_level[node_index][0], second_level[node_index][1], sigma_rr))
    sigma_first = []
    for node_index in range(4):
        sigma_rr = extract(sigma_second[node_index // 2], selector(map_mid[node_index], order_two // BLK))
        sigma_first.append(inverse(first_level[node_index][0], first_level[node_index][1], sigma_rr))
    pieces = []
    for subtree in range(N_LEAF):
        pieces.append(extract(sigma_first[subtree // members], selector(map_leaf[subtree], order_one // BLK)))
    return jnp.concatenate(pieces, axis=0)
```

```python
import functools

import jax
import jax.numpy as jnp
from jax import lax
from jax.experimental import pallas as pl
from jax.experimental.pallas import tpu as pltpu
from jax.sharding import Mesh, PartitionSpec as P

BLK = 128
SUB = 8
AXES = ("top", "mid", "member", "front")
LEAF = AXES[:3]
VMEM_BYTES = 48 * 1024 * 1024


def swap(block, axis, distance=1):
    count = lax.axis_size(axis)
    return lax.ppermute(block, axis, [(i, i ^ distance) for i in range(count)])


def dot(left, right):
    return jnp.dot(left, right, precision=lax.Precision.HIGHEST, preferred_element_type=jnp.float32)


def dot_nt(left, right):
    dims = (((1,), (1,)), ((), ()))
    return lax.dot_general(
        left, right, dims, precision=lax.Precision.HIGHEST, preferred_element_type=jnp.float32
    )


def block(index):
    return pl.ds(pl.multiple_of(index * BLK, BLK), BLK)


def inverse_of_block(rows):
    rows = list(rows)
    shape = rows[0].shape
    row_id = lax.broadcasted_iota(jnp.int32, shape, 0)
    lane_id = lax.broadcasted_iota(jnp.int32, shape, 1)
    for p in range(len(rows)):
        first = SUB * p
        panel = rows[p]
        columns = [
            jnp.broadcast_to(panel[:, first + j:first + j + 1], shape) for j in range(SUB)
        ]
        for j in range(SUB):
            pivot = jnp.broadcast_to(columns[j][j:j + 1, :], shape)
            scale = pltpu.reciprocal(pivot, approx=True)
            scale = scale * (2.0 - pivot * scale)
            here = row_id == j
            panel = jnp.where(lane_id == first + j, jnp.where(here, 1.0, 0.0), panel)
            factor = jnp.where(here, 0.0, columns[j])
            pivot_row = jnp.broadcast_to(panel[j:j + 1, :], shape) * scale
            panel = jnp.where(here, pivot_row, panel - factor * pivot_row)
            for m in range(j + 1, SUB):
                entry = jnp.broadcast_to(columns[m][j:j + 1, :], shape) * scale
                columns[m] = jnp.where(here, entry, columns[m] - factor * entry)
        own = (lane_id >= first) & (lane_id < first + SUB)
        spread = [jnp.broadcast_to(panel[k:k + 1, :], shape) for k in range(SUB)]
        for step in range(1, len(rows)):
            i = (p + step) % len(rows)
            total = jnp.where(own, 0.0, rows[i])
            for k in range(SUB):
                column = jnp.broadcast_to(rows[i][:, first + k:first + k + 1], shape)
                total = total - column * spread[k]
            rows[i] = total
        rows[p] = panel
    return rows


def invert(ref):
    order = ref.shape[0]
    blocks = order // BLK

    def step(k, carry):
        here = block(k)
        rows = [
            ref[pl.ds(pl.multiple_of(k * BLK + SUB * i, SUB), SUB), here]
            for i in range(BLK // SUB)
        ]
        inverse = jnp.concatenate(inverse_of_block(rows), axis=0)
        column = lax.broadcasted_iota(jnp.int32, (BLK, order), 1)
        own = (column >= k * BLK) & (column < (k + 1) * BLK)
        ref[here, here] = inverse
        scaled = jnp.where(own, 0.0, dot(inverse, jnp.where(own, 0.0, ref[here, :])))
        ref[here, :] = jnp.where(own, ref[here, :], scaled)
        spread = ref[here, :]

        def update(t, inner):
            i = t + (t >= k).astype(jnp.int32)
            row = ref[block(i), :]
            ref[block(i), :] = jnp.where(own, 0.0, row) - dot(ref[block(i), here], spread)
            return inner

        lax.fori_loop(0, blocks - 1, update, 0)
        return carry

    lax.fori_loop(0, blocks, step, 0)


def add_blocks(target, update, row_map, row):
    count = row_map.shape[1]
    for i in range(count):
        for j in range(count):
            rows, cols = block(row_map[row, i]), block(row_map[row, j])
            target[rows, cols] += update[i * BLK:(i + 1) * BLK, j * BLK:(j + 1) * BLK]


def selection(target, solved, row_map, row, sep):
    count = row_map.shape[1]
    shape = (BLK, target.shape[1])
    row_id = lax.broadcasted_iota(jnp.int32, shape, 0)
    lane_id = lax.broadcasted_iota(jnp.int32, shape, 1)
    for i in range(count):
        m = row_map[row, i]
        inside = m < sep
        source = solved[block(jnp.where(inside, m, 0)), :]
        unit = (lane_id - row_id == (m - sep) * BLK).astype(jnp.float32)
        target[i * BLK:(i + 1) * BLK, :] = jnp.where(inside, -source, unit)


def picked_inverse(inverse, row_map, row, i, j, sep):
    a, b = row_map[row, i], row_map[row, j]
    inside = (a < sep) & (b < sep)
    value = inverse[block(jnp.where(inside, a, 0)), block(jnp.where(inside, b, 0))]
    return jnp.where(inside, value, 0.0)


def node_index():
    return 2 * lax.axis_index("top") + lax.axis_index("mid")


def first_level(front, x_ref, t_ref, u_ref):
    sep = x_ref.shape[0]
    x_ref[...] = front[:sep, :sep]
    invert(x_ref)
    t_ref[...] = dot(x_ref[...], front[:sep, sep:])
    u_ref[...] = front[sep:, sep:] - dot(front[sep:, :sep], t_ref[...])


def second_level(entries, mine, other, top, map_mid, map_top, x_ref, t_ref, s_ref, k_ref,
                 front, cross, low):
    sep = x_ref.shape[0]
    node = lax.axis_index("top")
    child = node_index()
    front[...] = entries[pl.ds(pl.multiple_of(node * front.shape[0], BLK), front.shape[0]), :]
    add_blocks(front, mine, map_mid, child)
    add_blocks(front, other, map_mid, child + 1 - 2 * lax.axis_index("mid"))
    x_ref[...] = front[:sep, :sep]
    invert(x_ref)
    t_ref[...] = dot(x_ref[...], front[:sep, sep:])
    s_ref[...] = front[sep:, sep:] - dot(front[sep:, :sep], t_ref[...])
    count = map_top.shape[1]
    for i in range(count):
        for j in range(count):
            rows, cols = slice(i * BLK, (i + 1) * BLK), slice(j * BLK, (j + 1) * BLK)
            own = block(map_top[node, j])
            s_ref[rows, cols] += top[block(map_top[node, i]), own]
            cross[rows, cols] = top[block(map_top[1 - node, i]), own]
    low[...] = s_ref[...]
    invert(low)
    k_ref[...] = dot_nt(dot(cross[...], low[...]), cross[...])


def downward(s_ref, k_ref, x2, t2, x1, t1, map_mid, map_leaf, out, sigma, picker, work):
    sep2, sep1 = x2.shape[0] // BLK, x1.shape[0] // BLK
    child = node_index()
    members = lax.axis_size("member")
    leaf = child * members + lax.axis_index("member")
    column = lax.axis_index("front")
    sigma[...] = s_ref[...] - k_ref[...]
    invert(sigma)
    selection(picker, t2, map_mid, child, sep2)
    work[...] = dot_nt(dot(picker[...], sigma[...]), picker[...])
    count = map_mid.shape[1]
    for i in range(count):
        for j in range(count):
            rows, cols = slice(i * BLK, (i + 1) * BLK), slice(j * BLK, (j + 1) * BLK)
            sigma[rows, cols] = work[rows, cols] + picked_inverse(x2, map_mid, child, i, j, sep2)
    selection(picker, t1, map_leaf, leaf, sep1)
    width = out.shape[1]
    mine = picker[pl.ds(pl.multiple_of(column * width, BLK), width), :]
    result = dot(picker[...], dot_nt(sigma[...], mine))
    for i in range(map_leaf.shape[1]):
        for j in range(width // BLK):
            rows, cols = slice(i * BLK, (i + 1) * BLK), slice(j * BLK, (j + 1) * BLK)
            extra = picked_inverse(x1, map_leaf, leaf, i, column * (width // BLK) + j, sep1)
            out[rows, cols] = result[rows, cols] + extra


def square(order):
    return jax.ShapeDtypeStruct((order, order), jnp.float32)


def call(kernel, arrays, tables, outputs, scratch=()):
    vmem = pl.BlockSpec(memory_space=pltpu.VMEM)
    smem = pl.BlockSpec(memory_space=pltpu.SMEM)
    return pl.pallas_call(
        kernel,
        out_shape=outputs,
        in_specs=[vmem] * len(arrays) + [smem] * len(tables),
        out_specs=jax.tree.map(lambda _: vmem, outputs),
        scratch_shapes=[pltpu.VMEM(s.shape, s.dtype) for s in scratch],
        compiler_params=pltpu.CompilerParams(vmem_limit_bytes=VMEM_BYTES),
    )(*arrays, *tables)


def extend(update, block_list, parent_blocks):
    count = block_list.shape[0]
    hits = (block_list[:, None] == jnp.arange(parent_blocks)[None, :]).astype(jnp.int32)
    source = jnp.sum(hits * jnp.arange(count, dtype=jnp.int32)[:, None], axis=0)
    present = jnp.sum(hits, axis=0).astype(jnp.float32)
    blocked = update.reshape(count, BLK, count, BLK)
    picked = jnp.take(jnp.take(blocked, source, axis=0), source, axis=2)
    picked = picked * (present[:, None, None, None] * present[None, None, :, None])
    return picked.reshape(parent_blocks * BLK, parent_blocks * BLK)


def assemble(leaf_update, entries, map_leaf):
    members = lax.axis_size("member")
    member = lax.axis_index("member")
    column = lax.axis_index("front")
    leaf = node_index() * members + member
    update = lax.all_gather(leaf_update, "front", axis=1, tiled=True)
    rows, width = entries.shape
    order = rows * members
    spread = extend(update, map_leaf[leaf], order // BLK)
    share = lax.dynamic_slice_in_dim(spread, column * width, width, 1)
    own = lax.dynamic_slice_in_dim(share, member * rows, rows, 0) + entries
    share = lax.dynamic_update_slice_in_dim(share, own, member * rows, 0)
    distance = 1
    while distance < members:
        share = share + swap(share, "member", distance)
        distance *= 2
    return lax.all_gather(share, "front", axis=1, tiled=True)


def body(leaf_update, entries1, entries2, entries3, map_leaf, map_mid, map_top):
    low = map_mid.shape[1] * BLK
    sep1 = entries1.shape[0] * lax.axis_size("member") - low
    sep2 = entries2.shape[1] - map_top.shape[1] * BLK
    rest = map_top.shape[1] * BLK
    front_one = assemble(leaf_update, entries1, map_leaf)
    x1, t1, u1 = call(
        first_level, [front_one], [],
        (square(sep1), jax.ShapeDtypeStruct((sep1, low), jnp.float32), square(low)),
    )
    fronts = lax.axis_size("front")
    column = lax.axis_index("front")
    half = low // 2
    upper = column % 2
    sent = lax.dynamic_slice_in_dim(u1, upper * half, half, 0)
    got = swap(sent, "mid")
    pair = swap(got, "front")
    other = jnp.concatenate(
        [jnp.where(upper == 0, got, pair), jnp.where(upper == 0, pair, got)], axis=0
    )
    x2, t2, s, k = call(
        second_level, [entries2, u1, other, entries3], [map_mid, map_top],
        (square(sep2), jax.ShapeDtypeStruct((sep2, rest), jnp.float32), square(rest), square(rest)),
        [square(sep2 + rest), square(rest), square(rest)],
    )
    quarter = rest // 4
    part = upper + 2 * lax.axis_index("mid")
    sent = lax.dynamic_slice_in_dim(k, part * quarter, quarter, 0)
    got = swap(sent, "top")
    mid = lax.axis_index("mid")
    pair = swap(got, "mid")
    both = jnp.stack([jnp.where(mid == 0, got, pair), jnp.where(mid == 0, pair, got)])
    pair = swap(both, "front")
    halves = jnp.stack([jnp.where(upper == 0, both, pair), jnp.where(upper == 0, pair, both)], axis=1)
    k_other = halves.reshape(rest, rest)
    return call(
        downward, [s, k_other, x2, t2, x1, t1], [map_mid, map_leaf],
        jax.ShapeDtypeStruct(leaf_update.shape, jnp.float32),
        [square(rest), jax.ShapeDtypeStruct((low, rest), jnp.float32), square(low)],
    )


def solution(mesh):
    leaves = mesh.shape["leaf"]
    fronts = mesh.shape["front"]
    grid = Mesh(mesh.devices.reshape(2, 2, leaves // 4, fronts), AXES)
    in_specs = (P(LEAF, "front"), P(LEAF, "front"), P(), P(), P(), P(), P())
    return jax.shard_map(
        body, mesh=grid, in_specs=in_specs, out_specs=P(LEAF, "front"), check_vma=False
    )
```

```python
import functools

import jax
import jax.numpy as jnp
from jax import lax
from jax.experimental import pallas as pl
from jax.experimental.pallas import tpu as pltpu
from jax.sharding import Mesh, PartitionSpec as P

BLK = 128
SUB = 8
AXES = ("top", "mid", "member", "front")
LEAF = AXES[:3]
VMEM_BYTES = 48 * 1024 * 1024


def swap(block, axis, distance=1):
    count = lax.axis_size(axis)
    return lax.ppermute(block, axis, [(i, i ^ distance) for i in range(count)])


def dot(left, right):
    return jnp.dot(left, right, precision=lax.Precision.HIGHEST, preferred_element_type=jnp.float32)


def dot_nt(left, right):
    dims = (((1,), (1,)), ((), ()))
    return lax.dot_general(
        left, right, dims, precision=lax.Precision.HIGHEST, preferred_element_type=jnp.float32
    )


def block(index):
    return pl.ds(pl.multiple_of(index * BLK, BLK), BLK)


def inverse_of_block(rows):
    rows = list(rows)
    shape = rows[0].shape
    row_id = lax.broadcasted_iota(jnp.int32, shape, 0)
    lane_id = lax.broadcasted_iota(jnp.int32, shape, 1)
    for p in range(len(rows)):
        first = SUB * p
        panel = rows[p]
        columns = [
            jnp.broadcast_to(panel[:, first + j:first + j + 1], shape) for j in range(SUB)
        ]
        for j in range(SUB):
            pivot = jnp.broadcast_to(columns[j][j:j + 1, :], shape)
            scale = pltpu.reciprocal(pivot, approx=True)
            scale = scale * (2.0 - pivot * scale)
            here = row_id == j
            panel = jnp.where(lane_id == first + j, jnp.where(here, 1.0, 0.0), panel)
            factor = jnp.where(here, 0.0, columns[j])
            pivot_row = jnp.broadcast_to(panel[j:j + 1, :], shape) * scale
            panel = jnp.where(here, pivot_row, panel - factor * pivot_row)
            for m in range(j + 1, SUB):
                entry = jnp.broadcast_to(columns[m][j:j + 1, :], shape) * scale
                columns[m] = jnp.where(here, entry, columns[m] - factor * entry)
        own = (lane_id >= first) & (lane_id < first + SUB)
        spread = [jnp.broadcast_to(panel[k:k + 1, :], shape) for k in range(SUB)]
        for step in range(1, len(rows)):
            i = (p + step) % len(rows)
            total = jnp.where(own, 0.0, rows[i])
            for k in range(SUB):
                column = jnp.broadcast_to(rows[i][:, first + k:first + k + 1], shape)
                total = total - column * spread[k]
            rows[i] = total
        rows[p] = panel
    return rows


def invert(ref):
    order = ref.shape[0]
    blocks = order // BLK

    def step(k, carry):
        here = block(k)
        rows = [
            ref[pl.ds(pl.multiple_of(k * BLK + SUB * i, SUB), SUB), here]
            for i in range(BLK // SUB)
        ]
        inverse = jnp.concatenate(inverse_of_block(rows), axis=0)
        column = lax.broadcasted_iota(jnp.int32, (BLK, order), 1)
        own = (column >= k * BLK) & (column < (k + 1) * BLK)
        ref[here, here] = inverse
        scaled = jnp.where(own, 0.0, dot(inverse, jnp.where(own, 0.0, ref[here, :])))
        ref[here, :] = jnp.where(own, ref[here, :], scaled)
        spread = ref[here, :]

        def update(t, inner):
            i = t + (t >= k).astype(jnp.int32)
            row = ref[block(i), :]
            ref[block(i), :] = jnp.where(own, 0.0, row) - dot(ref[block(i), here], spread)
            return inner

        lax.fori_loop(0, blocks - 1, update, 0)
        return carry

    lax.fori_loop(0, blocks, step, 0)


def triangle(row, column):
    return row * (row + 1) // 2 + column


def lower_blocks(count):
    return [(i, j) for i in range(count) for j in range(i + 1)]


def packed_block(packed, index):
    return packed[pl.ds(pl.multiple_of(index * BLK, BLK), BLK), :]


def unpack(target, packed, first, count):
    for i, j in lower_blocks(count):
        value = packed_block(packed, first + triangle(i, j))
        rows, cols = slice(i * BLK, (i + 1) * BLK), slice(j * BLK, (j + 1) * BLK)
        target[rows, cols] = value
        if i != j:
            target[cols, rows] = value.T


def pack(target, full, count):
    for i, j in lower_blocks(count):
        place = triangle(i, j) * BLK
        target[place:place + BLK, :] = full[i * BLK:(i + 1) * BLK, j * BLK:(j + 1) * BLK]


def add_blocks(target, packed, row_map, row):
    for i, j in lower_blocks(row_map.shape[1]):
        a, b = block(row_map[row, i]), block(row_map[row, j])
        value = packed_block(packed, triangle(i, j))
        target[a, b] += value
        if i != j:
            target[b, a] += value.T


def selection(target, solved, row_map, row, sep):
    count = row_map.shape[1]
    shape = (BLK, target.shape[1])
    row_id = lax.broadcasted_iota(jnp.int32, shape, 0)
    lane_id = lax.broadcasted_iota(jnp.int32, shape, 1)
    for i in range(count):
        m = row_map[row, i]
        inside = m < sep
        source = solved[block(jnp.where(inside, m, 0)), :]
        unit = (lane_id - row_id == (m - sep) * BLK).astype(jnp.float32)
        target[i * BLK:(i + 1) * BLK, :] = jnp.where(inside, -source, unit)


def picked_inverse(inverse, row_map, row, i, j, sep):
    a, b = row_map[row, i], row_map[row, j]
    inside = (a < sep) & (b < sep)
    value = inverse[block(jnp.where(inside, a, 0)), block(jnp.where(inside, b, 0))]
    return jnp.where(inside, value, 0.0)


def node_index():
    return 2 * lax.axis_index("top") + lax.axis_index("mid")


def contribute(leaf_update, entries, map_leaf, ss_keep, ss_send, rest_keep, rest_send, packed):
    members = lax.axis_size("member")
    member = lax.axis_index("member")
    column = lax.axis_index("front")
    upper = column % 2
    leaf = node_index() * members + member
    packed[...] = jnp.zeros(packed.shape, packed.dtype)
    rows, width = entries.shape
    height = min(rows, BLK)
    for i in range(rows // height):
        start = member * rows + i * height
        r = start // BLK
        for j in range(width // BLK):
            c = column * (width // BLK) + j

            @pl.when(r >= c)
            def _():
                place = pl.multiple_of(triangle(r, c) * BLK + start % BLK, height)
                packed[pl.ds(place, height), :] = (
                    entries[i * height:(i + 1) * height, j * BLK:(j + 1) * BLK]
                )

    width = leaf_update.shape[1] // BLK
    for j in range(width):
        c = map_leaf[leaf, column * width + j]
        for i in range(map_leaf.shape[1]):
            r = map_leaf[leaf, i]

            @pl.when(r >= c)
            def _():
                place = block(triangle(r, c))
                packed[place, :] += leaf_update[i * BLK:(i + 1) * BLK, j * BLK:(j + 1) * BLK]

    first = 2 * ss_keep.shape[0]
    for keep, send, start in ((ss_keep, ss_send, 0), (rest_keep, rest_send, first)):
        half = keep.shape[0]
        keep[...] = packed[pl.ds(pl.multiple_of(start + upper * half, SUB), half), :]
        send[...] = packed[pl.ds(pl.multiple_of(start + (1 - upper) * half, SUB), half), :]


def join(target, parts, upper):
    size = parts[0].shape[0]
    for p in range(4):
        side = upper if p < 2 else 1 - upper
        start = pl.multiple_of((2 * side + p % 2) * size, SUB)
        target[pl.ds(start, size), :] = parts[2 * p][...] + parts[2 * p + 1][...]


def first_inverse(*refs):
    parts, (x_ref, packed) = refs[:8], refs[8:]
    join(packed, parts, lax.axis_index("front") % 2)
    unpack(x_ref, packed, 0, x_ref.shape[0] // BLK)
    invert(x_ref)


def first_update(*refs):
    x_ref, parts, (t_ref, u_ref, send, packed, rs, rr) = refs[0], refs[1:9], refs[9:]
    upper = lax.axis_index("front") % 2
    join(packed, parts, upper)
    sep, low = x_ref.shape[0] // BLK, rr.shape[0] // BLK
    first = triangle(sep, 0)
    for i in range(low):
        for j in range(sep):
            rs[i * BLK:(i + 1) * BLK, j * BLK:(j + 1) * BLK] = packed_block(
                packed, triangle(sep + i, j) - first
            )
        for j in range(i + 1):
            rows, cols = slice(i * BLK, (i + 1) * BLK), slice(j * BLK, (j + 1) * BLK)
            value = packed_block(packed, triangle(sep + i, sep + j) - first)
            rr[rows, cols] = value
            if i != j:
                rr[cols, rows] = value.T
    t_ref[...] = dot_nt(x_ref[...], rs[...])
    rr[...] -= dot(rs[...], t_ref[...])
    pack(u_ref, rr, low)
    half = send.shape[0]
    send[...] = u_ref[pl.ds(pl.multiple_of(upper * half, SUB), half), :]


def second_level(entries, mine, got, pair, top, map_mid, map_top, x_ref, t_ref, s_ref, send,
                 front, cross, low, packed):
    sep = x_ref.shape[0]
    node = lax.axis_index("top")
    mid = lax.axis_index("mid")
    upper = lax.axis_index("front") % 2
    child = node_index()
    front[...] = entries[pl.ds(pl.multiple_of(node * front.shape[0], BLK), front.shape[0]), :]
    half = got.shape[0]
    packed[pl.ds(pl.multiple_of(upper * half, SUB), half), :] = got[...]
    packed[pl.ds(pl.multiple_of((1 - upper) * half, SUB), half), :] = pair[...]
    add_blocks(front, mine, map_mid, child)
    add_blocks(front, packed, map_mid, child + 1 - 2 * mid)
    x_ref[...] = front[:sep, :sep]
    invert(x_ref)
    t_ref[...] = dot(x_ref[...], front[:sep, sep:])
    s_ref[...] = front[sep:, sep:] - dot(front[sep:, :sep], t_ref[...])
    count = map_top.shape[1]
    for i in range(count):
        for j in range(count):
            rows, cols = slice(i * BLK, (i + 1) * BLK), slice(j * BLK, (j + 1) * BLK)
            own = block(map_top[node, j])
            s_ref[rows, cols] += top[block(map_top[node, i]), own]
            cross[rows, cols] = top[block(map_top[1 - node, i]), own]
    low[...] = s_ref[...]
    invert(low)
    low[...] = dot_nt(dot(cross[...], low[...]), cross[...])
    pack(packed, low, count)
    part = send.shape[0]
    send[...] = packed[pl.ds(pl.multiple_of((2 * mid + upper) * part, SUB), part), :]


def downward(s_ref, k00, k01, k10, k11, x2, t2, x1, t1, map_mid, map_leaf, out, sigma, picker, work, packed):
    sep2, sep1 = x2.shape[0] // BLK, x1.shape[0] // BLK
    child = node_index()
    members = lax.axis_size("member")
    leaf = child * members + lax.axis_index("member")
    column = lax.axis_index("front")
    mid, upper = lax.axis_index("mid"), column % 2
    for piece, m, u in ((k00, mid, upper), (k01, 1 - mid, upper),
                        (k10, mid, 1 - upper), (k11, 1 - mid, 1 - upper)):
        part = piece.shape[0]
        packed[pl.ds(pl.multiple_of((2 * m + u) * part, SUB), part), :] = piece[...]
    unpack(work, packed, 0, work.shape[0] // BLK)
    sigma[...] = s_ref[...] - work[...]
    invert(sigma)
    selection(picker, t2, map_mid, child, sep2)
    work[...] = dot_nt(dot(picker[...], sigma[...]), picker[...])
    count = map_mid.shape[1]
    for i in range(count):
        for j in range(count):
            rows, cols = slice(i * BLK, (i + 1) * BLK), slice(j * BLK, (j + 1) * BLK)
            sigma[rows, cols] = work[rows, cols] + picked_inverse(x2, map_mid, child, i, j, sep2)
    selection(picker, t1, map_leaf, leaf, sep1)
    width = out.shape[1]
    mine = picker[pl.ds(pl.multiple_of(column * width, BLK), width), :]
    result = dot(picker[...], dot_nt(sigma[...], mine))
    for i in range(map_leaf.shape[1]):
        for j in range(width // BLK):
            rows, cols = slice(i * BLK, (i + 1) * BLK), slice(j * BLK, (j + 1) * BLK)
            extra = picked_inverse(x1, map_leaf, leaf, i, column * (width // BLK) + j, sep1)
            out[rows, cols] = result[rows, cols] + extra


def square(order):
    return jax.ShapeDtypeStruct((order, order), jnp.float32)


def call(kernel, arrays, tables, outputs, scratch=()):
    vmem = pl.BlockSpec(memory_space=pltpu.VMEM)
    smem = pl.BlockSpec(memory_space=pltpu.SMEM)
    return pl.pallas_call(
        kernel,
        out_shape=outputs,
        in_specs=[vmem] * len(arrays) + [smem] * len(tables),
        out_specs=jax.tree.map(lambda _: vmem, outputs),
        scratch_shapes=[pltpu.VMEM(s.shape, s.dtype) for s in scratch],
        compiler_params=pltpu.CompilerParams(vmem_limit_bytes=VMEM_BYTES),
    )(*arrays, *tables)


def strip(rows):
    return jax.ShapeDtypeStruct((rows, BLK), jnp.float32)


def spread_sum(keep, send, after=None):
    total = keep + swap(send, "front")
    size = total.shape[0] // 2
    pieces = [total[:size], total[size:]]
    steps = [("front", 1 << b) for b in range(1, lax.axis_size("front").bit_length() - 1)]
    steps += [("member", 1 << b) for b in range(lax.axis_size("member").bit_length() - 1)]
    if after is not None:
        pieces, _ = lax.optimization_barrier((pieces, after))
    marker = None
    for number in range(len(steps)):
        got = [swap(pieces[0], *steps[number]), swap(pieces[1], *steps[-1 - number])]
        if number == 0:
            marker = got
        if number < len(steps) - 1:
            pieces = [pieces[0] + got[0], pieces[1] + got[1]]
    own = [pieces[0], got[0], pieces[1], got[1]]
    return own + [swap(value, "front") for value in own], marker


def body(leaf_update, entries1, entries2, entries3, map_leaf, map_mid, map_top):
    low = map_mid.shape[1] * BLK
    sep1 = entries1.shape[0] * lax.axis_size("member") - low
    sep2 = entries2.shape[1] - map_top.shape[1] * BLK
    rest = map_top.shape[1] * BLK
    first = triangle(sep1 // BLK, 0) * BLK
    total = triangle((sep1 + low) // BLK, 0) * BLK
    halves = [strip(n // 2) for n in (first, first, total - first, total - first)]
    ss_keep, ss_send, rest_keep, rest_send = call(
        contribute, [leaf_update, entries1], [map_leaf], halves, [strip(total)]
    )
    ss_parts, marker = spread_sum(ss_keep, ss_send)
    rest_parts, _ = spread_sum(rest_keep, rest_send, marker)
    x1 = call(first_inverse, ss_parts, [], square(sep1), [strip(first)])
    update = triangle(low // BLK, 0) * BLK
    t1, u1, sent = call(
        first_update, [x1] + rest_parts, [],
        (jax.ShapeDtypeStruct((sep1, low), jnp.float32), strip(update), strip(update // 2)),
        [strip(total - first), jax.ShapeDtypeStruct((low, sep1), jnp.float32), square(low)],
    )
    got = swap(sent, "mid")
    pair = swap(got, "front")
    schur = triangle(rest // BLK, 0) * BLK
    x2, t2, s, sent = call(
        second_level, [entries2, u1, got, pair, entries3], [map_mid, map_top],
        (square(sep2), jax.ShapeDtypeStruct((sep2, rest), jnp.float32), square(rest),
         strip(schur // 4)),
        [square(sep2 + rest), square(rest), square(rest), strip(max(update, schur))],
    )
    got = swap(sent, "top")
    pair = swap(got, "mid")
    pieces = [got, pair, swap(got, "front"), swap(pair, "front")]
    return call(
        downward, [s] + pieces + [x2, t2, x1, t1], [map_mid, map_leaf],
        jax.ShapeDtypeStruct(leaf_update.shape, jnp.float32),
        [square(rest), jax.ShapeDtypeStruct((low, rest), jnp.float32), square(low), strip(schur)],
    )


def solution(mesh):
    leaves = mesh.shape["leaf"]
    fronts = mesh.shape["front"]
    grid = Mesh(mesh.devices.reshape(2, 2, leaves // 4, fronts), AXES)
    in_specs = (P(LEAF, "front"), P(LEAF, "front"), P(), P(), P(), P(), P())
    return jax.shard_map(
        body, mesh=grid, in_specs=in_specs, out_specs=P(LEAF, "front"), check_vma=False
    )
```

```python
import functools

import jax
import jax.numpy as jnp
from jax import lax
from jax.experimental import pallas as pl
from jax.experimental.pallas import tpu as pltpu
from jax.sharding import Mesh, PartitionSpec as P

BLK = 128
SUB = 8
AXES = ("top", "mid", "member", "front")
LEAF = AXES[:3]
VMEM_BYTES = 48 * 1024 * 1024
COST = 40_000_000


def swap(block, axis, distance=1):
    count = lax.axis_size(axis)
    return lax.ppermute(block, axis, [(i, i ^ distance) for i in range(count)])


def dot(left, right):
    return jnp.dot(left, right, precision=lax.Precision.HIGHEST, preferred_element_type=jnp.float32)


def dot_nt(left, right):
    dims = (((1,), (1,)), ((), ()))
    return lax.dot_general(
        left, right, dims, precision=lax.Precision.HIGHEST, preferred_element_type=jnp.float32
    )


def block(index):
    return pl.ds(pl.multiple_of(index * BLK, BLK), BLK)


def inverse_of_block(rows):
    rows = list(rows)
    shape = rows[0].shape
    row_id = lax.broadcasted_iota(jnp.int32, shape, 0)
    lane_id = lax.broadcasted_iota(jnp.int32, shape, 1)
    for p in range(len(rows)):
        first = SUB * p
        panel = rows[p]
        columns = [
            jnp.broadcast_to(panel[:, first + j:first + j + 1], shape) for j in range(SUB)
        ]
        for j in range(SUB):
            pivot = jnp.broadcast_to(columns[j][j:j + 1, :], shape)
            scale = pltpu.reciprocal(pivot, approx=True)
            scale = scale * (2.0 - pivot * scale)
            here = row_id == j
            panel = jnp.where(lane_id == first + j, jnp.where(here, 1.0, 0.0), panel)
            factor = jnp.where(here, 0.0, columns[j])
            pivot_row = jnp.broadcast_to(panel[j:j + 1, :], shape) * scale
            panel = jnp.where(here, pivot_row, panel - factor * pivot_row)
            for m in range(j + 1, SUB):
                entry = jnp.broadcast_to(columns[m][j:j + 1, :], shape) * scale
                columns[m] = jnp.where(here, entry, columns[m] - factor * entry)
        own = (lane_id >= first) & (lane_id < first + SUB)
        spread = [jnp.broadcast_to(panel[k:k + 1, :], shape) for k in range(SUB)]
        for step in range(1, len(rows)):
            i = (p + step) % len(rows)
            total = jnp.where(own, 0.0, rows[i])
            for k in range(SUB):
                column = jnp.broadcast_to(rows[i][:, first + k:first + k + 1], shape)
                total = total - column * spread[k]
            rows[i] = total
        rows[p] = panel
    return rows


def invert(ref, start=0, stop=None):
    order = ref.shape[0]
    blocks = order // BLK
    stop = blocks if stop is None else stop

    def step(k, carry):
        here = block(k)
        rows = [
            ref[pl.ds(pl.multiple_of(k * BLK + SUB * i, SUB), SUB), here]
            for i in range(BLK // SUB)
        ]
        inverse = jnp.concatenate(inverse_of_block(rows), axis=0)
        column = lax.broadcasted_iota(jnp.int32, (BLK, order), 1)
        own = (column >= k * BLK) & (column < (k + 1) * BLK)
        ref[here, here] = inverse
        scaled = jnp.where(own, 0.0, dot(inverse, jnp.where(own, 0.0, ref[here, :])))
        ref[here, :] = jnp.where(own, ref[here, :], scaled)
        spread = ref[here, :]

        def update(t, inner):
            i = t + (t >= k).astype(jnp.int32)
            row = ref[block(i), :]
            ref[block(i), :] = jnp.where(own, 0.0, row) - dot(ref[block(i), here], spread)
            return inner

        lax.fori_loop(0, blocks - 1, update, 0)
        return carry

    lax.fori_loop(start, stop, step, 0)


def triangle(row, column):
    return row * (row + 1) // 2 + column


def lower_blocks(count):
    return [(i, j) for i in range(count) for j in range(i + 1)]


def packed_block(packed, index):
    return packed[pl.ds(pl.multiple_of(index * BLK, BLK), BLK), :]


def unpack(target, packed, first, count):
    for i, j in lower_blocks(count):
        value = packed_block(packed, first + triangle(i, j))
        rows, cols = slice(i * BLK, (i + 1) * BLK), slice(j * BLK, (j + 1) * BLK)
        target[rows, cols] = value
        if i != j:
            target[cols, rows] = value.T


def pack(target, full, count):
    for i, j in lower_blocks(count):
        place = triangle(i, j) * BLK
        target[place:place + BLK, :] = full[i * BLK:(i + 1) * BLK, j * BLK:(j + 1) * BLK]


def add_blocks(target, packed, row_map, row):
    for i, j in lower_blocks(row_map.shape[1]):
        a, b = block(row_map[row, i]), block(row_map[row, j])
        value = packed_block(packed, triangle(i, j))
        target[a, b] += value
        if i != j:
            target[b, a] += value.T


def selection(target, solved, row_map, row, sep):
    count = row_map.shape[1]
    shape = (BLK, target.shape[1])
    row_id = lax.broadcasted_iota(jnp.int32, shape, 0)
    lane_id = lax.broadcasted_iota(jnp.int32, shape, 1)
    for i in range(count):
        m = row_map[row, i]
        inside = m < sep
        source = solved[block(jnp.where(inside, m, 0)), :]
        unit = (lane_id - row_id == (m - sep) * BLK).astype(jnp.float32)
        target[i * BLK:(i + 1) * BLK, :] = jnp.where(inside, -source, unit)


def picked_inverse(inverse, row_map, row, i, j, sep):
    a, b = row_map[row, i], row_map[row, j]
    inside = (a < sep) & (b < sep)
    value = inverse[block(jnp.where(inside, a, 0)), block(jnp.where(inside, b, 0))]
    return jnp.where(inside, value, 0.0)


def node_index():
    return 2 * lax.axis_index("top") + lax.axis_index("mid")


def contribute(leaf_update, entries, map_leaf, ss_keep, ss_send, rest_keep, rest_send, packed):
    members = lax.axis_size("member")
    member = lax.axis_index("member")
    column = lax.axis_index("front")
    upper = column % 2
    leaf = node_index() * members + member
    packed[...] = jnp.zeros(packed.shape, packed.dtype)
    rows, width = entries.shape
    height = min(rows, BLK)
    for i in range(rows // height):
        start = member * rows + i * height
        r = start // BLK
        for j in range(width // BLK):
            c = column * (width // BLK) + j

            @pl.when(r >= c)
            def _():
                place = pl.multiple_of(triangle(r, c) * BLK + start % BLK, height)
                packed[pl.ds(place, height), :] = (
                    entries[i * height:(i + 1) * height, j * BLK:(j + 1) * BLK]
                )

    width = leaf_update.shape[1] // BLK
    for j in range(width):
        c = map_leaf[leaf, column * width + j]
        for i in range(map_leaf.shape[1]):
            r = map_leaf[leaf, i]

            @pl.when(r >= c)
            def _():
                place = block(triangle(r, c))
                packed[place, :] += leaf_update[i * BLK:(i + 1) * BLK, j * BLK:(j + 1) * BLK]

    first = 2 * ss_keep.shape[0]
    for keep, send, start in ((ss_keep, ss_send, 0), (rest_keep, rest_send, first)):
        half = keep.shape[0]
        keep[...] = packed[pl.ds(pl.multiple_of(start + upper * half, SUB), half), :]
        send[...] = packed[pl.ds(pl.multiple_of(start + (1 - upper) * half, SUB), half), :]


def join(target, parts, upper):
    size = parts[0].shape[0]
    for p in range(4):
        side = upper if p < 2 else 1 - upper
        start = pl.multiple_of((2 * side + p % 2) * size, SUB)
        target[pl.ds(start, size), :] = parts[2 * p][...] + parts[2 * p + 1][...]


def first_inverse(*refs):
    parts, (x_ref, packed) = refs[:8], refs[8:]
    join(packed, parts, lax.axis_index("front") % 2)
    blocks = x_ref.shape[0] // BLK
    unpack(x_ref, packed, 0, blocks)
    invert(x_ref, 0, blocks // 2)


def first_inverse_end(half_ref, x_ref):
    x_ref[...] = half_ref[...]
    blocks = x_ref.shape[0] // BLK
    invert(x_ref, blocks // 2, blocks)


def first_update(*refs):
    x_ref, parts, (t_ref, u_ref, send, packed, rs, rr) = refs[0], refs[1:9], refs[9:]
    upper = lax.axis_index("front") % 2
    join(packed, parts, upper)
    sep, low = x_ref.shape[0] // BLK, rr.shape[0] // BLK
    first = triangle(sep, 0)
    for i in range(low):
        for j in range(sep):
            rs[i * BLK:(i + 1) * BLK, j * BLK:(j + 1) * BLK] = packed_block(
                packed, triangle(sep + i, j) - first
            )
        for j in range(i + 1):
            rows, cols = slice(i * BLK, (i + 1) * BLK), slice(j * BLK, (j + 1) * BLK)
            value = packed_block(packed, triangle(sep + i, sep + j) - first)
            rr[rows, cols] = value
            if i != j:
                rr[cols, rows] = value.T
    t_ref[...] = dot_nt(x_ref[...], rs[...])
    rr[...] -= dot(rs[...], t_ref[...])
    pack(u_ref, rr, low)
    half = send.shape[0]
    send[...] = u_ref[pl.ds(pl.multiple_of(upper * half, SUB), half), :]


def second_level(entries, mine, got, pair, top, map_mid, map_top, x_ref, t_ref, s_ref, send,
                 front, cross, low, packed):
    sep = x_ref.shape[0]
    node = lax.axis_index("top")
    mid = lax.axis_index("mid")
    upper = lax.axis_index("front") % 2
    child = node_index()
    front[...] = entries[pl.ds(pl.multiple_of(node * front.shape[0], BLK), front.shape[0]), :]
    half = got.shape[0]
    packed[pl.ds(pl.multiple_of(upper * half, SUB), half), :] = got[...]
    packed[pl.ds(pl.multiple_of((1 - upper) * half, SUB), half), :] = pair[...]
    add_blocks(front, mine, map_mid, child)
    add_blocks(front, packed, map_mid, child + 1 - 2 * mid)
    x_ref[...] = front[:sep, :sep]
    invert(x_ref)
    t_ref[...] = dot(x_ref[...], front[:sep, sep:])
    s_ref[...] = front[sep:, sep:] - dot(front[sep:, :sep], t_ref[...])
    count = map_top.shape[1]
    for i in range(count):
        for j in range(count):
            rows, cols = slice(i * BLK, (i + 1) * BLK), slice(j * BLK, (j + 1) * BLK)
            own = block(map_top[node, j])
            s_ref[rows, cols] += top[block(map_top[node, i]), own]
            cross[rows, cols] = top[block(map_top[1 - node, i]), own]
    low[...] = s_ref[...]
    invert(low)
    low[...] = dot_nt(dot(cross[...], low[...]), cross[...])
    pack(packed, low, count)
    part = send.shape[0]
    send[...] = packed[pl.ds(pl.multiple_of((2 * mid + upper) * part, SUB), part), :]


def downward(s_ref, k00, k01, k10, k11, x2, t2, x1, t1, map_mid, map_leaf, out, sigma, picker, work, packed):
    sep2, sep1 = x2.shape[0] // BLK, x1.shape[0] // BLK
    child = node_index()
    members = lax.axis_size("member")
    leaf = child * members + lax.axis_index("member")
    column = lax.axis_index("front")
    mid, upper = lax.axis_index("mid"), column % 2
    for piece, m, u in ((k00, mid, upper), (k01, 1 - mid, upper),
                        (k10, mid, 1 - upper), (k11, 1 - mid, 1 - upper)):
        part = piece.shape[0]
        packed[pl.ds(pl.multiple_of((2 * m + u) * part, SUB), part), :] = piece[...]
    unpack(work, packed, 0, work.shape[0] // BLK)
    sigma[...] = s_ref[...] - work[...]
    invert(sigma)
    selection(picker, t2, map_mid, child, sep2)
    work[...] = dot_nt(dot(picker[...], sigma[...]), picker[...])
    count = map_mid.shape[1]
    for i in range(count):
        for j in range(count):
            rows, cols = slice(i * BLK, (i + 1) * BLK), slice(j * BLK, (j + 1) * BLK)
            sigma[rows, cols] = work[rows, cols] + picked_inverse(x2, map_mid, child, i, j, sep2)
    selection(picker, t1, map_leaf, leaf, sep1)
    width = out.shape[1]
    mine = picker[pl.ds(pl.multiple_of(column * width, BLK), width), :]
    result = dot(picker[...], dot_nt(sigma[...], mine))
    for i in range(map_leaf.shape[1]):
        for j in range(width // BLK):
            rows, cols = slice(i * BLK, (i + 1) * BLK), slice(j * BLK, (j + 1) * BLK)
            extra = picked_inverse(x1, map_leaf, leaf, i, column * (width // BLK) + j, sep1)
            out[rows, cols] = result[rows, cols] + extra


def square(order):
    return jax.ShapeDtypeStruct((order, order), jnp.float32)


def call(kernel, arrays, tables, outputs, scratch=(), cost=0):
    vmem = pl.BlockSpec(memory_space=pltpu.VMEM)
    smem = pl.BlockSpec(memory_space=pltpu.SMEM)
    return pl.pallas_call(
        kernel,
        out_shape=outputs,
        in_specs=[vmem] * len(arrays) + [smem] * len(tables),
        out_specs=jax.tree.map(lambda _: vmem, outputs),
        scratch_shapes=[pltpu.VMEM(s.shape, s.dtype) for s in scratch],
        compiler_params=pltpu.CompilerParams(vmem_limit_bytes=VMEM_BYTES),
        cost_estimate=pl.CostEstimate(flops=cost, bytes_accessed=cost, transcendentals=0),
    )(*arrays, *tables)


def strip(rows):
    return jax.ShapeDtypeStruct((rows, BLK), jnp.float32)


def after(values, *others):
    return lax.optimization_barrier((values, others))[0]


def routes():
    fronts = lax.axis_size("front").bit_length() - 1
    members = lax.axis_size("member").bit_length() - 1
    return [("front", 1 << b) for b in range(1, fronts)] + [("member", 1 << b) for b in range(members)]


def crossing(pieces, number):
    steps = routes()
    return [swap(pieces[0], *steps[number]), swap(pieces[1], *steps[-1 - number])]


def cut(total):
    size = total.shape[0] // 2
    return [total[:size], total[size:]]


def add_pairs(pieces, got):
    return [pieces[0] + got[0], pieces[1] + got[1]]


def both_cores(pieces, got):
    own = [pieces[0], got[0], pieces[1], got[1]]
    return own + [swap(value, "front") for value in own]


def body(leaf_update, entries1, entries2, entries3, map_leaf, map_mid, map_top):
    low = map_mid.shape[1] * BLK
    sep1 = entries1.shape[0] * lax.axis_size("member") - low
    sep2 = entries2.shape[1] - map_top.shape[1] * BLK
    rest = map_top.shape[1] * BLK
    first = triangle(sep1 // BLK, 0) * BLK
    total = triangle((sep1 + low) // BLK, 0) * BLK
    halves = [strip(n // 2) for n in (first, first, total - first, total - first)]
    ss_keep, ss_send, rest_keep, rest_send = call(
        contribute, [leaf_update, entries1], [map_leaf], halves, [strip(total)]
    )
    last = len(routes()) - 1
    pieces = cut(ss_keep + swap(ss_send, "front"))
    for number in range(last):
        pieces = add_pairs(pieces, crossing(pieces, number))
    got = crossing(pieces, last)
    ss_parts = both_cores(pieces, got)
    rest_send = after(rest_send, pieces)
    pieces = cut(rest_keep + swap(rest_send, "front"))
    pieces = after(pieces, got)
    got = crossing(pieces, 0)
    state = call(first_inverse, ss_parts, [], square(sep1), [strip(first)], COST)
    for number in range(1, last + 1):
        pieces = add_pairs(pieces, after(got, state))
        got = crossing(pieces, number)
    x1 = call(first_inverse_end, [state], [], square(sep1), [], COST)
    got = after(got, x1)
    rest_parts = both_cores(pieces, got)
    update = triangle(low // BLK, 0) * BLK
    t1, u1, sent = call(
        first_update, [x1] + rest_parts, [],
        (jax.ShapeDtypeStruct((sep1, low), jnp.float32), strip(update), strip(update // 2)),
        [strip(total - first), jax.ShapeDtypeStruct((low, sep1), jnp.float32), square(low)],
    )
    got = swap(sent, "mid")
    pair = swap(got, "front")
    schur = triangle(rest // BLK, 0) * BLK
    x2, t2, s, sent = call(
        second_level, [entries2, u1, got, pair, entries3], [map_mid, map_top],
        (square(sep2), jax.ShapeDtypeStruct((sep2, rest), jnp.float32), square(rest),
         strip(schur // 4)),
        [square(sep2 + rest), square(rest), square(rest), strip(max(update, schur))],
    )
    got = swap(sent, "top")
    pair = swap(got, "mid")
    pieces = [got, pair, swap(got, "front"), swap(pair, "front")]
    return call(
        downward, [s] + pieces + [x2, t2, x1, t1], [map_mid, map_leaf],
        jax.ShapeDtypeStruct(leaf_update.shape, jnp.float32),
        [square(rest), jax.ShapeDtypeStruct((low, rest), jnp.float32), square(low), strip(schur)],
    )


def solution(mesh):
    leaves = mesh.shape["leaf"]
    fronts = mesh.shape["front"]
    grid = Mesh(mesh.devices.reshape(2, 2, leaves // 4, fronts), AXES)
    in_specs = (P(LEAF, "front"), P(LEAF, "front"), P(), P(), P(), P(), P())
    return jax.shard_map(
        body, mesh=grid, in_specs=in_specs, out_specs=P(LEAF, "front"), check_vma=False
    )
```

```python
import functools

import jax
import jax.numpy as jnp
from jax import lax
from jax.experimental import pallas as pl
from jax.experimental.pallas import tpu as pltpu
from jax.sharding import Mesh, PartitionSpec as P

BLK = 128
SUB = 8
AXES = ("top", "mid", "member", "front")
LEAF = AXES[:3]
VMEM_BYTES = 48 * 1024 * 1024
COST = 40_000_000


def swap(block, axis, distance=1):
    count = lax.axis_size(axis)
    return lax.ppermute(block, axis, [(i, i ^ distance) for i in range(count)])


def dot(left, right):
    return jnp.dot(left, right, precision=lax.Precision.HIGHEST, preferred_element_type=jnp.float32)


def dot_nt(left, right):
    dims = (((1,), (1,)), ((), ()))
    return lax.dot_general(
        left, right, dims, precision=lax.Precision.HIGHEST, preferred_element_type=jnp.float32
    )


def dot_tn(left, right):
    dims = (((0,), (0,)), ((), ()))
    return lax.dot_general(
        left, right, dims, precision=lax.Precision.HIGHEST, preferred_element_type=jnp.float32
    )


def block(index):
    return pl.ds(pl.multiple_of(index * BLK, BLK), BLK)


def column_of(panel, index):
    return jnp.broadcast_to(panel[:, index:index + 1], panel.shape)


def row_of(panel, index):
    return jnp.broadcast_to(panel[index:index + 1, :], panel.shape)


def minus_sum(value, terms):
    terms = list(terms)
    while len(terms) > 1:
        pairs = [terms[i] + terms[i + 1] for i in range(0, len(terms) - 1, 2)]
        terms = pairs + terms[2 * len(pairs):]
    return value - terms[0]


def eliminate_panel(columns, panel, ahead, row_id):
    columns, ahead = list(columns), list(ahead)
    pivot = row_of(columns[0], 0)
    for j in range(SUB):
        here = row_id == j
        scale = 1.0 / pivot
        factor = jnp.where(here, 0.0, columns[j]) * scale
        for m in range(j + 1, SUB):
            entry = row_of(columns[m], j)
            value = columns[m] - factor * entry
            if m == j + 1:
                pivot = row_of(value, m)
            columns[m] = jnp.where(here, entry * scale, value)
        for m in range(len(ahead)):
            entry = row_of(ahead[m], j)
            ahead[m] = jnp.where(here, entry * scale, ahead[m] - factor * entry)
        entry = row_of(panel, j)
        panel = jnp.where(here, entry * scale, panel - factor * entry)
    return panel, ahead


def eliminate_block(rows, between=()):
    rows = list(rows)
    count = len(rows)
    shape = rows[0].shape
    row_id = lax.broadcasted_iota(jnp.int32, shape, 0)
    lane_id = lax.broadcasted_iota(jnp.int32, shape, 1)
    slots = [(piece * (count - 4)) // max(len(between) - 1, 1) for piece in range(len(between))]
    before, scaled = [], []
    half = count // 2
    for start in (0, half):
        end = start + half
        left, right = [], []
        columns = [column_of(rows[start], SUB * start + j) for j in range(SUB)]
        for p in range(start, end):
            panel = rows[p]
            first, last = SUB * p, SUB * (p + 1)
            own = (lane_id >= first) & (lane_id < last)
            unit = (lane_id == first + row_id).astype(jnp.float32)
            before.append(jnp.where(lane_id < first, panel, unit))
            left.append(panel)
            ahead = []
            if p + 1 < end:
                ahead = [column_of(panel, last + j) for j in range(SUB)]
            panel, ahead = eliminate_panel(columns, jnp.where(own, unit, panel), ahead, row_id)
            scaled.append(jnp.where(lane_id < last, panel, 0.0))
            right.append(jnp.where((lane_id < last) | (lane_id >= SUB * end), panel, 0.0))
            if p + 1 < end:
                spread = [row_of(panel, k) for k in range(SUB)]
                near = [column_of(rows[p + 1], first + k) for k in range(SUB)]
                columns = [
                    minus_sum(
                        column_of(rows[p + 1], last + j),
                        [near[k] * row_of(ahead[j], k) for k in range(SUB)],
                    )
                    for j in range(SUB)
                ]
                for i in range(p + 1, end):
                    if i > p + 1:
                        near = [column_of(rows[i], first + k) for k in range(SUB)]
                    rows[i] = minus_sum(
                        jnp.where(own, 0.0, rows[i]), [near[k] * spread[k] for k in range(SUB)]
                    )
            for piece, slot in zip(between, slots):
                if slot == p:
                    piece()
        if end < count:
            change = dot_tn(jnp.concatenate(left, axis=0), jnp.concatenate(right, axis=0))
            inside = (lane_id >= SUB * start) & (lane_id < SUB * end)
            for i in range(end, count):
                rows[i] = jnp.where(inside, 0.0, rows[i]) - change[SUB * i:SUB * (i + 1), :]
    return jnp.concatenate(before, axis=0), jnp.concatenate(scaled, axis=0)


def inverse_scratch(order):
    return [strip(BLK)] * 4 + [jax.ShapeDtypeStruct((BLK, order), jnp.float32)]


def invert(ref, work, start=0, stop=None):
    pivot, before, scaled, inverse, spread = work
    order = ref.shape[0]
    blocks = order // BLK
    stop = blocks if stop is None else stop

    def panels():
        return [pivot[SUB * i:SUB * (i + 1), :] for i in range(BLK // SUB)]

    def look_ahead(k, result):
        before[...], scaled[...] = result
        after_k = jnp.minimum(k + 1, blocks - 1)
        cross = ref[block(k), block(after_k)]
        change = dot_tn(dot(result[0], cross), dot(result[1], cross))
        pivot[...] = ref[block(after_k), block(after_k)] - change

    def update(k):
        here = block(k)
        lane_id = lax.broadcasted_iota(jnp.int32, (BLK, order), 1)
        row_id = lax.broadcasted_iota(jnp.int32, (BLK, order), 0)
        own = (lane_id >= k * BLK) & (lane_id < (k + 1) * BLK)

        def form():
            inverse[...] = dot_tn(before[...], scaled[...])

        def scale():
            unit = (lane_id - row_id == k * BLK).astype(jnp.float32)
            spread[...] = dot(inverse[...], jnp.where(own, unit, ref[here, :]))

        def change(i):
            rows = slice(i * BLK, (i + 1) * BLK)
            factor = jnp.where(k == i, 0.0, ref[rows, here])
            value = jnp.where(own, 0.0, ref[rows, :]) - dot(factor, spread[...])
            ref[rows, :] = jnp.where(k == i, spread[...], value)

        return [form, scale] + [functools.partial(change, i) for i in range(blocks)]

    def step(k, carry):
        look_ahead(k, eliminate_block(panels(), update(k - 1)))
        return carry

    pivot[...] = ref[block(start), block(start)]
    look_ahead(start, eliminate_block(panels()))
    lax.fori_loop(start + 1, stop, step, 0)
    for piece in update(stop - 1):
        piece()


def triangle(row, column):
    return row * (row + 1) // 2 + column


def lower_blocks(count):
    return [(i, j) for i in range(count) for j in range(i + 1)]


def packed_block(packed, index):
    return packed[pl.ds(pl.multiple_of(index * BLK, BLK), BLK), :]


def unpack(target, packed, first, count):
    for i, j in lower_blocks(count):
        value = packed_block(packed, first + triangle(i, j))
        rows, cols = slice(i * BLK, (i + 1) * BLK), slice(j * BLK, (j + 1) * BLK)
        target[rows, cols] = value
        if i != j:
            target[cols, rows] = value.T


def pack(target, full, count):
    for i, j in lower_blocks(count):
        place = triangle(i, j) * BLK
        target[place:place + BLK, :] = full[i * BLK:(i + 1) * BLK, j * BLK:(j + 1) * BLK]


def core_share(count, upper):
    assert count == 4
    a, b = 3 * upper, 1 + upper
    return [(a, a), ((a + 1) % 4, a), ((a + 2) % 4, a), (b, b), (b + 1, b)]


def add_blocks(target, packed, row_map, row):
    count = row_map.shape[1]
    for place, (i, j) in enumerate(core_share(count, 0) + core_share(count, 1)):
        a, b = block(row_map[row, i]), block(row_map[row, j])
        value = packed_block(packed, place)
        target[a, b] += value
        if i != j:
            target[b, a] += value.T


def selection(target, solved, row_map, row, sep):
    count = row_map.shape[1]
    shape = (BLK, target.shape[1])
    row_id = lax.broadcasted_iota(jnp.int32, shape, 0)
    lane_id = lax.broadcasted_iota(jnp.int32, shape, 1)
    for i in range(count):
        m = row_map[row, i]
        inside = m < sep
        source = solved[block(jnp.where(inside, m, 0)), :]
        unit = (lane_id - row_id == (m - sep) * BLK).astype(jnp.float32)
        target[i * BLK:(i + 1) * BLK, :] = jnp.where(inside, -source, unit)


def picked_inverse(inverse, row_map, row, i, j, sep):
    a, b = row_map[row, i], row_map[row, j]
    inside = (a < sep) & (b < sep)
    value = inverse[block(jnp.where(inside, a, 0)), block(jnp.where(inside, b, 0))]
    return jnp.where(inside, value, 0.0)


def node_index():
    return 2 * lax.axis_index("top") + lax.axis_index("mid")


def contribute(leaf_update, entries, map_leaf, ss_keep, ss_send, rest_keep, rest_send, packed):
    members = lax.axis_size("member")
    member = lax.axis_index("member")
    column = lax.axis_index("front")
    upper = column % 2
    leaf = node_index() * members + member
    packed[...] = jnp.zeros(packed.shape, packed.dtype)
    rows, width = entries.shape
    height = min(rows, BLK)
    for i in range(rows // height):
        start = member * rows + i * height
        r = start // BLK
        for j in range(width // BLK):
            c = column * (width // BLK) + j

            @pl.when(r >= c)
            def _():
                place = pl.multiple_of(triangle(r, c) * BLK + start % BLK, height)
                packed[pl.ds(place, height), :] = (
                    entries[i * height:(i + 1) * height, j * BLK:(j + 1) * BLK]
                )

    width = leaf_update.shape[1] // BLK
    for j in range(width):
        c = map_leaf[leaf, column * width + j]
        for i in range(map_leaf.shape[1]):
            r = map_leaf[leaf, i]

            @pl.when(r >= c)
            def _():
                place = block(triangle(r, c))
                packed[place, :] += leaf_update[i * BLK:(i + 1) * BLK, j * BLK:(j + 1) * BLK]

    first = 2 * ss_keep.shape[0]
    for keep, send, start in ((ss_keep, ss_send, 0), (rest_keep, rest_send, first)):
        half = keep.shape[0]
        keep[...] = packed[pl.ds(pl.multiple_of(start + upper * half, SUB), half), :]
        send[...] = packed[pl.ds(pl.multiple_of(start + (1 - upper) * half, SUB), half), :]


def join(target, parts, upper):
    size = parts[0].shape[0]
    for p in range(4):
        side = upper if p < 2 else 1 - upper
        start = pl.multiple_of((2 * side + p % 2) * size, SUB)
        target[pl.ds(start, size), :] = parts[2 * p][...] + parts[2 * p + 1][...]


def first_inverse(*refs):
    parts, (x_ref, packed, *work) = refs[:8], refs[8:]
    join(packed, parts, lax.axis_index("front") % 2)
    blocks = x_ref.shape[0] // BLK
    unpack(x_ref, packed, 0, blocks)
    invert(x_ref, work, 0, blocks // 2)


def first_inverse_end(half_ref, x_ref, *work):
    x_ref[...] = half_ref[...]
    blocks = x_ref.shape[0] // BLK
    invert(x_ref, work, blocks // 2, blocks)


def first_update(*refs):
    x_ref, parts, (rs, send, packed) = refs[0], refs[1:9], refs[9:]
    upper = lax.axis_index("front") % 2
    join(packed, parts, upper)
    sep, low = x_ref.shape[0] // BLK, rs.shape[0] // BLK
    first = triangle(sep, 0)
    for i in range(low):
        for j in range(sep):
            rs[i * BLK:(i + 1) * BLK, j * BLK:(j + 1) * BLK] = packed_block(
                packed, triangle(sep + i, j) - first
            )
    for side in range(2):

        @pl.when(upper == side)
        def _():
            share = core_share(low, side)
            columns = sorted({j for _, j in share})
            rows = jnp.concatenate([rs[j * BLK:(j + 1) * BLK, :] for j in columns], axis=0)
            solved = dot_nt(x_ref[...], rows)
            for place, (i, j) in enumerate(share):
                number = triangle(sep + max(i, j), sep + min(i, j)) - first
                value = packed_block(packed, number)
                value = value if i >= j else value.T
                at = columns.index(j) * BLK
                change = dot(rs[i * BLK:(i + 1) * BLK, :], solved[:, at:at + BLK])
                send[place * BLK:(place + 1) * BLK, :] = value - change


def second_level(entries, mine, pair, got, got_pair, top, map_mid, map_top, x_ref, t_ref, s_ref,
                 send, front, cross, low, packed, *work):
    sep = x_ref.shape[0]
    node = lax.axis_index("top")
    mid = lax.axis_index("mid")
    upper = lax.axis_index("front") % 2
    child = node_index()
    front[...] = entries[pl.ds(pl.multiple_of(node * front.shape[0], BLK), front.shape[0]), :]
    half = got.shape[0]
    for own, other, source in ((mine, pair, child), (got, got_pair, child + 1 - 2 * mid)):
        packed[pl.ds(pl.multiple_of(upper * half, SUB), half), :] = own[...]
        packed[pl.ds(pl.multiple_of((1 - upper) * half, SUB), half), :] = other[...]
        add_blocks(front, packed, map_mid, source)
    x_ref[...] = front[:sep, :sep]
    invert(x_ref, work)
    t_ref[...] = dot(x_ref[...], front[:sep, sep:])
    s_ref[...] = front[sep:, sep:] - dot(front[sep:, :sep], t_ref[...])
    count = map_top.shape[1]
    for i in range(count):
        for j in range(count):
            rows, cols = slice(i * BLK, (i + 1) * BLK), slice(j * BLK, (j + 1) * BLK)
            own = block(map_top[node, j])
            s_ref[rows, cols] += top[block(map_top[node, i]), own]
            cross[rows, cols] = top[block(map_top[1 - node, i]), own]
    low[...] = s_ref[...]
    invert(low, work)
    part = 2 * mid + upper
    solved = dot(cross[block(part), :], low[...])
    send[:BLK, :] = dot_nt(solved, cross[block(part), :])
    send[BLK:2 * BLK, :] = dot_nt(solved, cross[block((part + 1) % count), :])
    far = dot_nt(solved, cross[block((part + 2) % count), :])
    start = jnp.where(part < count // 2, 0, BLK // 2)
    packed[:BLK, :] = jnp.where(part < count // 2, far, far.T)
    send[2 * BLK:, :] = packed[pl.ds(pl.multiple_of(start, SUB), BLK // 2), :]


def prepare(x1, rs, x2, t2, map_mid, map_leaf, chain, constant, t1, near, far, picked):
    sep2, sep1 = x2.shape[0] // BLK, x1.shape[0] // BLK
    child = node_index()
    leaf = child * lax.axis_size("member") + lax.axis_index("member")
    column = lax.axis_index("front")
    t1[...] = dot_nt(x1[...], rs[...])
    selection(near, t1, map_leaf, leaf, sep1)
    selection(far, t2, map_mid, child, sep2)
    chain[...] = dot(near[...], far[...])
    count = map_mid.shape[1]
    for i in range(count):
        for j in range(count):
            rows, cols = slice(i * BLK, (i + 1) * BLK), slice(j * BLK, (j + 1) * BLK)
            picked[rows, cols] = picked_inverse(x2, map_mid, child, i, j, sep2)
    width = constant.shape[1]
    mine = near[pl.ds(pl.multiple_of(column * width, BLK), width), :]
    constant[...] = dot(near[...], dot_nt(picked[...], mine))
    for i in range(map_leaf.shape[1]):
        for j in range(width // BLK):
            rows, cols = slice(i * BLK, (i + 1) * BLK), slice(j * BLK, (j + 1) * BLK)
            place = column * (width // BLK) + j
            constant[rows, cols] += picked_inverse(x1, map_leaf, leaf, i, place, sep1)


def downward(s_ref, k00, k01, k10, k11, chain, constant, out, sigma, packed, *work):
    column = lax.axis_index("front")
    mid, upper = lax.axis_index("mid"), column % 2
    count = sigma.shape[0] // BLK
    for piece, m, u in ((k00, mid, upper), (k01, 1 - mid, upper),
                        (k10, mid, 1 - upper), (k11, 1 - mid, 1 - upper)):
        size = piece.shape[0]
        packed[pl.ds(pl.multiple_of((2 * m + u) * size, SUB), size), :] = piece[...]
    sigma[...] = s_ref[...]
    size = k00.shape[0]
    for m in range(count):
        pieces = [((m, m), 0, BLK, 0), ((m, (m + 1) % count), BLK, BLK, 0)]
        if m < count // 2:
            pieces.append(((m, m + 2), 2 * BLK, BLK // 2, 0))
        else:
            pieces.append(((m - 2, m), 2 * BLK, BLK // 2, BLK // 2))
        for (i, j), start, rows, offset in pieces:
            value = packed[m * size + start:m * size + start + rows, :]
            first = i * BLK + offset
            sigma[first:first + rows, j * BLK:(j + 1) * BLK] -= value
            if i != j:
                sigma[j * BLK:(j + 1) * BLK, first:first + rows] -= value.T
    invert(sigma, work)
    width = out.shape[1]
    mine = chain[pl.ds(pl.multiple_of(column * width, BLK), width), :]
    out[...] = dot(chain[...], dot_nt(sigma[...], mine)) + constant[...]


def square(order):
    return jax.ShapeDtypeStruct((order, order), jnp.float32)


def call(kernel, arrays, tables, outputs, scratch=(), cost=0):
    vmem = pl.BlockSpec(memory_space=pltpu.VMEM)
    smem = pl.BlockSpec(memory_space=pltpu.SMEM)
    return pl.pallas_call(
        kernel,
        out_shape=outputs,
        in_specs=[vmem] * len(arrays) + [smem] * len(tables),
        out_specs=jax.tree.map(lambda _: vmem, outputs),
        scratch_shapes=[pltpu.VMEM(s.shape, s.dtype) for s in scratch],
        compiler_params=pltpu.CompilerParams(vmem_limit_bytes=VMEM_BYTES),
        cost_estimate=pl.CostEstimate(flops=cost, bytes_accessed=cost, transcendentals=0),
    )(*arrays, *tables)


def strip(rows):
    return jax.ShapeDtypeStruct((rows, BLK), jnp.float32)


def after(values, *others):
    return lax.optimization_barrier((values, others))[0]


def routes():
    fronts = lax.axis_size("front").bit_length() - 1
    members = lax.axis_size("member").bit_length() - 1
    return [("front", 1 << b) for b in range(1, fronts)] + [("member", 1 << b) for b in range(members)]


def crossing(pieces, number):
    steps = routes()
    return [swap(pieces[0], *steps[number]), swap(pieces[1], *steps[-1 - number])]


def cut(total):
    size = total.shape[0] // 2
    return [total[:size], total[size:]]


def add_pairs(pieces, got):
    return [pieces[0] + got[0], pieces[1] + got[1]]


def both_cores(pieces, got):
    own = [pieces[0], got[0], pieces[1], got[1]]
    return own + [swap(value, "front") for value in own]


def body(leaf_update, entries1, entries2, entries3, map_leaf, map_mid, map_top):
    low = map_mid.shape[1] * BLK
    sep1 = entries1.shape[0] * lax.axis_size("member") - low
    sep2 = entries2.shape[1] - map_top.shape[1] * BLK
    rest = map_top.shape[1] * BLK
    first = triangle(sep1 // BLK, 0) * BLK
    total = triangle((sep1 + low) // BLK, 0) * BLK
    halves = [strip(n // 2) for n in (first, first, total - first, total - first)]
    ss_keep, ss_send, rest_keep, rest_send = call(
        contribute, [leaf_update, entries1], [map_leaf], halves, [strip(total)]
    )
    last = len(routes()) - 1
    pieces = cut(ss_keep + swap(ss_send, "front"))
    for number in range(last):
        pieces = add_pairs(pieces, crossing(pieces, number))
    got = crossing(pieces, last)
    ss_parts = both_cores(pieces, got)
    rest_send = after(rest_send, pieces)
    pieces = cut(rest_keep + swap(rest_send, "front"))
    pieces = after(pieces, got)
    got = crossing(pieces, 0)
    state = call(
        first_inverse, ss_parts, [], square(sep1), [strip(first)] + inverse_scratch(sep1), COST
    )
    for number in range(1, last + 1):
        pieces = add_pairs(pieces, after(got, state))
        got = crossing(pieces, number)
    x1 = call(first_inverse_end, [state], [], square(sep1), inverse_scratch(sep1), COST)
    got = after(got, x1)
    rest_parts = both_cores(pieces, got)
    update = triangle(low // BLK, 0) * BLK
    rs, sent = call(
        first_update, [x1] + rest_parts, [],
        (jax.ShapeDtypeStruct((low, sep1), jnp.float32), strip(update // 2)),
        [strip(total - first)], COST,
    )
    got = swap(sent, "mid")
    shares = [sent, swap(sent, "front"), got, swap(got, "front")]
    schur = triangle(rest // BLK, 0) * BLK
    x2, t2, s, sent = call(
        second_level, [entries2] + shares + [entries3], [map_mid, map_top],
        (square(sep2), jax.ShapeDtypeStruct((sep2, rest), jnp.float32), square(rest),
         strip(schur // 4)),
        [square(sep2 + rest), square(rest), square(rest), strip(max(update, schur))]
        + inverse_scratch(sep2), 2 * COST,
    )
    got = swap(sent, "top")
    chain, constant = call(
        prepare, [x1, rs, x2, t2], [map_mid, map_leaf],
        (jax.ShapeDtypeStruct((low, rest), jnp.float32),
         jax.ShapeDtypeStruct(leaf_update.shape, jnp.float32)),
        [jax.ShapeDtypeStruct((sep1, low), jnp.float32), square(low),
         jax.ShapeDtypeStruct((low, rest), jnp.float32), square(low)], COST // 2,
    )
    got = after(got, chain)
    pair = swap(got, "mid")
    pieces = [got, pair, swap(got, "front"), swap(pair, "front")]
    return call(
        downward, [s] + pieces + [chain, constant], [],
        jax.ShapeDtypeStruct(leaf_update.shape, jnp.float32),
        [square(rest), strip(schur)] + inverse_scratch(rest), COST,
    )


def solution(mesh):
    leaves = mesh.shape["leaf"]
    fronts = mesh.shape["front"]
    grid = Mesh(mesh.devices.reshape(2, 2, leaves // 4, fronts), AXES)
    in_specs = (P(LEAF, "front"), P(LEAF, "front"), P(), P(), P(), P(), P())
    return jax.shard_map(
        body, mesh=grid, in_specs=in_specs, out_specs=P(LEAF, "front"), check_vma=False
    )
```

```python
import functools

import jax
import jax.numpy as jnp
from jax import lax
from jax.experimental import pallas as pl
from jax.experimental.pallas import tpu as pltpu
from jax.sharding import Mesh, PartitionSpec as P

BLK = 128
SUB = 8
AXES = ("top", "mid", "member", "front")
LEAF = AXES[:3]
VMEM_BYTES = 48 * 1024 * 1024
COST = 40_000_000


def swap(block, axis, distance=1):
    count = lax.axis_size(axis)
    return lax.ppermute(block, axis, [(i, i ^ distance) for i in range(count)])


def dot(left, right):
    return jnp.dot(left, right, precision=lax.Precision.HIGHEST, preferred_element_type=jnp.float32)


def dot_nt(left, right):
    dims = (((1,), (1,)), ((), ()))
    return lax.dot_general(
        left, right, dims, precision=lax.Precision.HIGHEST, preferred_element_type=jnp.float32
    )


def dot_tn(left, right):
    dims = (((0,), (0,)), ((), ()))
    return lax.dot_general(
        left, right, dims, precision=lax.Precision.HIGHEST, preferred_element_type=jnp.float32
    )


def block(index):
    return pl.ds(pl.multiple_of(index * BLK, BLK), BLK)


def column_of(panel, index):
    return jnp.broadcast_to(panel[:, index:index + 1], panel.shape)


def row_of(panel, index):
    return jnp.broadcast_to(panel[index:index + 1, :], panel.shape)


def minus_sum(value, terms):
    terms = list(terms)
    while len(terms) > 1:
        pairs = [terms[i] + terms[i + 1] for i in range(0, len(terms) - 1, 2)]
        terms = pairs + terms[2 * len(pairs):]
    return value - terms[0]


def eliminate_panel(columns, panel, ahead, row_id):
    columns, ahead = list(columns), list(ahead)
    pivot = row_of(columns[0], 0)
    for j in range(SUB):
        here = row_id == j
        scale = 1.0 / pivot
        factor = jnp.where(here, 0.0, columns[j]) * scale
        for m in range(j + 1, SUB):
            entry = row_of(columns[m], j)
            value = columns[m] - factor * entry
            if m == j + 1:
                pivot = row_of(value, m)
            columns[m] = jnp.where(here, entry * scale, value)
        for m in range(len(ahead)):
            entry = row_of(ahead[m], j)
            ahead[m] = jnp.where(here, entry * scale, ahead[m] - factor * entry)
        entry = row_of(panel, j)
        panel = jnp.where(here, entry * scale, panel - factor * entry)
    return panel, ahead


def eliminate_block(rows, between=()):
    rows = list(rows)
    count = len(rows)
    shape = rows[0].shape
    row_id = lax.broadcasted_iota(jnp.int32, shape, 0)
    lane_id = lax.broadcasted_iota(jnp.int32, shape, 1)
    slots = [(piece * (count - 4)) // max(len(between) - 1, 1) for piece in range(len(between))]
    before, scaled = [], []
    half = count // 2
    for start in (0, half):
        end = start + half
        left, right = [], []
        columns = [column_of(rows[start], SUB * start + j) for j in range(SUB)]
        for p in range(start, end):
            panel = rows[p]
            first, last = SUB * p, SUB * (p + 1)
            own = (lane_id >= first) & (lane_id < last)
            unit = (lane_id == first + row_id).astype(jnp.float32)
            before.append(jnp.where(lane_id < first, panel, unit))
            left.append(panel)
            ahead = []
            if p + 1 < end:
                ahead = [column_of(panel, last + j) for j in range(SUB)]
            panel, ahead = eliminate_panel(columns, jnp.where(own, unit, panel), ahead, row_id)
            scaled.append(jnp.where(lane_id < last, panel, 0.0))
            right.append(jnp.where((lane_id < last) | (lane_id >= SUB * end), panel, 0.0))
            if p + 1 < end:
                spread = [row_of(panel, k) for k in range(SUB)]
                near = [column_of(rows[p + 1], first + k) for k in range(SUB)]
                columns = [
                    minus_sum(
                        column_of(rows[p + 1], last + j),
                        [near[k] * row_of(ahead[j], k) for k in range(SUB)],
                    )
                    for j in range(SUB)
                ]
                for i in range(p + 1, end):
                    if i > p + 1:
                        near = [column_of(rows[i], first + k) for k in range(SUB)]
                    rows[i] = minus_sum(
                        jnp.where(own, 0.0, rows[i]), [near[k] * spread[k] for k in range(SUB)]
                    )
            for piece, slot in zip(between, slots):
                if slot == p:
                    piece()
        if end < count:
            change = dot_tn(jnp.concatenate(left, axis=0), jnp.concatenate(right, axis=0))
            inside = (lane_id >= SUB * start) & (lane_id < SUB * end)
            for i in range(end, count):
                rows[i] = jnp.where(inside, 0.0, rows[i]) - change[SUB * i:SUB * (i + 1), :]
    return jnp.concatenate(before, axis=0), jnp.concatenate(scaled, axis=0)


def inverse_scratch(width):
    return [strip(BLK)] * 4 + [jax.ShapeDtypeStruct((BLK, width), jnp.float32)]


def invert(ref, work, start=0, stop=None, solve=False):
    pivot, before, scaled, inverse, spread = work
    order, width = ref.shape
    blocks = order // BLK
    stop = blocks if stop is None else stop

    def panels():
        return [pivot[SUB * i:SUB * (i + 1), :] for i in range(BLK // SUB)]

    def look_ahead(k, result):
        before[...], scaled[...] = result
        after_k = jnp.minimum(k + 1, blocks - 1)
        cross = ref[block(k), block(after_k)]
        change = dot_tn(dot(result[0], cross), dot(result[1], cross))
        pivot[...] = ref[block(after_k), block(after_k)] - change

    def update(k, first=0):
        here, cols = block(k), slice(first, width)
        shape = (BLK, width - first)
        lane_id = lax.broadcasted_iota(jnp.int32, shape, 1) + first
        row_id = lax.broadcasted_iota(jnp.int32, shape, 0)
        own = (lane_id >= k * BLK) & (lane_id < (k + 1) * BLK)

        def form():
            inverse[...] = dot_tn(before[...], scaled[...])

        def scale():
            unit = (lane_id - row_id == k * BLK).astype(jnp.float32)
            spread[:, cols] = dot(inverse[...], jnp.where(own, unit, ref[here, cols]))

        def change(i):
            rows = slice(i * BLK, (i + 1) * BLK)
            factor = jnp.where(k == i, 0.0, ref[rows, here])
            value = jnp.where(own, 0.0, ref[rows, cols]) - dot(factor, spread[:, cols])
            ref[rows, cols] = jnp.where(k == i, spread[:, cols], value)

        return [form, scale] + [functools.partial(change, i) for i in range(blocks)]

    def step(k, carry):
        look_ahead(k, eliminate_block(panels(), update(k - 1)))
        return carry

    pivot[...] = ref[block(start), block(start)]
    look_ahead(start, eliminate_block(panels()))
    lax.fori_loop(start + 1, stop, step, 0)
    for piece in update(stop - 1, order if solve else 0):
        piece()


def triangle(row, column):
    return row * (row + 1) // 2 + column


def lower_blocks(count):
    return [(i, j) for i in range(count) for j in range(i + 1)]


def packed_block(packed, index):
    return packed[pl.ds(pl.multiple_of(index * BLK, BLK), BLK), :]


def unpack(target, packed, first, count):
    for i, j in lower_blocks(count):
        value = packed_block(packed, first + triangle(i, j))
        rows, cols = slice(i * BLK, (i + 1) * BLK), slice(j * BLK, (j + 1) * BLK)
        target[rows, cols] = value
        if i != j:
            target[cols, rows] = value.T


def pack(target, full, count):
    for i, j in lower_blocks(count):
        place = triangle(i, j) * BLK
        target[place:place + BLK, :] = full[i * BLK:(i + 1) * BLK, j * BLK:(j + 1) * BLK]


def core_share(count, upper):
    assert count == 4
    a, b = 3 * upper, 1 + upper
    return [(a, a), ((a + 1) % 4, a), ((a + 2) % 4, a), (b, b), (b + 1, b)]


def add_blocks(target, packed, row_map, row):
    count = row_map.shape[1]
    for place, (i, j) in enumerate(core_share(count, 0) + core_share(count, 1)):
        a, b = block(row_map[row, i]), block(row_map[row, j])
        value = packed_block(packed, place)
        target[a, b] += value
        if i != j:
            target[b, a] += value.T


def selection(target, solved, row_map, row, sep):
    count = row_map.shape[1]
    shape = (BLK, target.shape[1])
    row_id = lax.broadcasted_iota(jnp.int32, shape, 0)
    lane_id = lax.broadcasted_iota(jnp.int32, shape, 1)
    for i in range(count):
        m = row_map[row, i]
        inside = m < sep
        source = solved[block(jnp.where(inside, m, 0)), :]
        unit = (lane_id - row_id == (m - sep) * BLK).astype(jnp.float32)
        target[i * BLK:(i + 1) * BLK, :] = jnp.where(inside, -source, unit)


def picked_inverse(inverse, row_map, row, i, j, sep):
    a, b = row_map[row, i], row_map[row, j]
    inside = (a < sep) & (b < sep)
    value = inverse[block(jnp.where(inside, a, 0)), block(jnp.where(inside, b, 0))]
    return jnp.where(inside, value, 0.0)


def node_index():
    return 2 * lax.axis_index("top") + lax.axis_index("mid")


def contribute(leaf_update, entries, map_leaf, ss_keep, ss_send, rest_keep, rest_send, packed):
    members = lax.axis_size("member")
    member = lax.axis_index("member")
    column = lax.axis_index("front")
    upper = column % 2
    leaf = node_index() * members + member
    packed[...] = jnp.zeros(packed.shape, packed.dtype)
    rows, width = entries.shape
    height = min(rows, BLK)
    for i in range(rows // height):
        start = member * rows + i * height
        r = start // BLK
        for j in range(width // BLK):
            c = column * (width // BLK) + j

            @pl.when(r >= c)
            def _():
                place = pl.multiple_of(triangle(r, c) * BLK + start % BLK, height)
                packed[pl.ds(place, height), :] = (
                    entries[i * height:(i + 1) * height, j * BLK:(j + 1) * BLK]
                )

    width = leaf_update.shape[1] // BLK
    for j in range(width):
        c = map_leaf[leaf, column * width + j]
        for i in range(map_leaf.shape[1]):
            r = map_leaf[leaf, i]

            @pl.when(r >= c)
            def _():
                place = block(triangle(r, c))
                packed[place, :] += leaf_update[i * BLK:(i + 1) * BLK, j * BLK:(j + 1) * BLK]

    first = 2 * ss_keep.shape[0]
    for keep, send, start in ((ss_keep, ss_send, 0), (rest_keep, rest_send, first)):
        half = keep.shape[0]
        keep[...] = packed[pl.ds(pl.multiple_of(start + upper * half, SUB), half), :]
        send[...] = packed[pl.ds(pl.multiple_of(start + (1 - upper) * half, SUB), half), :]


def join(target, parts, upper):
    size = parts[0].shape[0]
    for p in range(4):
        side = upper if p < 2 else 1 - upper
        start = pl.multiple_of((2 * side + p % 2) * size, SUB)
        target[pl.ds(start, size), :] = parts[2 * p][...] + parts[2 * p + 1][...]


def first_inverse(*refs):
    parts, (x_ref, packed, *work) = refs[:8], refs[8:]
    join(packed, parts, lax.axis_index("front") % 2)
    blocks = x_ref.shape[0] // BLK
    unpack(x_ref, packed, 0, blocks)
    invert(x_ref, work, 0, blocks // 2)


def first_inverse_end(half_ref, x_ref, *work):
    x_ref[...] = half_ref[...]
    blocks = x_ref.shape[0] // BLK
    invert(x_ref, work, blocks // 2, blocks)


def first_update(*refs):
    x_ref, parts, (rs, send, packed) = refs[0], refs[1:9], refs[9:]
    upper = lax.axis_index("front") % 2
    join(packed, parts, upper)
    sep, low = x_ref.shape[0] // BLK, rs.shape[0] // BLK
    first = triangle(sep, 0)
    for i in range(low):
        for j in range(sep):
            rs[i * BLK:(i + 1) * BLK, j * BLK:(j + 1) * BLK] = packed_block(
                packed, triangle(sep + i, j) - first
            )
    for side in range(2):

        @pl.when(upper == side)
        def _():
            share = core_share(low, side)
            columns = sorted({j for _, j in share})
            rows = jnp.concatenate([rs[j * BLK:(j + 1) * BLK, :] for j in columns], axis=0)
            solved = dot_nt(x_ref[...], rows)
            for place, (i, j) in enumerate(share):
                number = triangle(sep + max(i, j), sep + min(i, j)) - first
                value = packed_block(packed, number)
                value = value if i >= j else value.T
                at = columns.index(j) * BLK
                change = dot(rs[i * BLK:(i + 1) * BLK, :], solved[:, at:at + BLK])
                send[place * BLK:(place + 1) * BLK, :] = value - change


def second_level(mine, pair, got, got_pair, entries, top, map_mid, map_top, x_ref, t_ref, s_ref,
                 send, front, cross, low, own_top, packed, *rest):
    *work, front_sem, sems = rest
    sep, order = x_ref.shape[0], front.shape[0]
    count = map_top.shape[1]
    node = lax.axis_index("top")
    mid = lax.axis_index("mid")
    upper = lax.axis_index("front") % 2
    child = node_index()
    part = 2 * mid + upper
    start = pl.multiple_of(node * order, BLK)
    front_copy = pltpu.make_async_copy(entries.at[pl.ds(start, order), :], front, front_sem)
    front_copy.start()
    copies = []

    def fetch(row, column, target, i, j):
        place = target.at[i * BLK:(i + 1) * BLK, j * BLK:(j + 1) * BLK]
        copy = pltpu.make_async_copy(top.at[block(row), block(column)], place, sems.at[len(copies)])
        copy.start()
        copies.append(copy)

    for i in range(count):
        for j in range(count):
            fetch(map_top[node, i], map_top[node, j], own_top, i, j)
            fetch(map_top[1 - node, i], map_top[node, j], cross, i, j)
        fetch(map_top[node, i], map_top[1 - node, part], low, i, count)
    front_copy.wait()
    half = got.shape[0]
    for own, other, source in ((mine, pair, child), (got, got_pair, child + 1 - 2 * mid)):
        packed[pl.ds(pl.multiple_of(upper * half, SUB), half), :] = own[...]
        packed[pl.ds(pl.multiple_of((1 - upper) * half, SUB), half), :] = other[...]
        add_blocks(front, packed, map_mid, source)
    invert(front.at[:sep, :], work)
    x_ref[...] = front[:sep, :sep]
    t_ref[...] = front[:sep, sep:]
    update = front[sep:, sep:] - dot(front[sep:, :sep], t_ref[...])
    for copy in copies:
        copy.wait()
    update += own_top[...]
    s_ref[...] = update
    low[:, :count * BLK] = update
    invert(low, work, solve=True)
    solved = low[:, count * BLK:]
    send[:BLK, :] = dot(cross[block(part), :], solved)
    send[BLK:2 * BLK, :] = dot(cross[block((part + 1) % count), :], solved)
    far = dot(cross[block((part + 2) % count), :], solved)
    start = jnp.where(part < count // 2, 0, BLK // 2)
    packed[:BLK, :] = jnp.where(part < count // 2, far, far.T)
    send[2 * BLK:, :] = packed[pl.ds(pl.multiple_of(start, SUB), BLK // 2), :]


def prepare(x1, rs, x2, t2, map_mid, map_leaf, chain, columns, constant, t1, near, far, picked):
    sep2, sep1 = x2.shape[0] // BLK, x1.shape[0] // BLK
    child = node_index()
    leaf = child * lax.axis_size("member") + lax.axis_index("member")
    column = lax.axis_index("front")
    t1[...] = dot_nt(x1[...], rs[...])
    selection(near, t1, map_leaf, leaf, sep1)
    selection(far, t2, map_mid, child, sep2)
    chain[...] = dot(near[...], far[...])
    count = map_mid.shape[1]
    for i in range(count):
        for j in range(count):
            rows, cols = slice(i * BLK, (i + 1) * BLK), slice(j * BLK, (j + 1) * BLK)
            picked[rows, cols] = picked_inverse(x2, map_mid, child, i, j, sep2)
    width = constant.shape[1]
    columns[...] = chain[pl.ds(pl.multiple_of(column * width, BLK), width), :].T
    mine = near[pl.ds(pl.multiple_of(column * width, BLK), width), :]
    constant[...] = dot(near[...], dot_nt(picked[...], mine))
    for i in range(map_leaf.shape[1]):
        for j in range(width // BLK):
            rows, cols = slice(i * BLK, (i + 1) * BLK), slice(j * BLK, (j + 1) * BLK)
            place = column * (width // BLK) + j
            constant[rows, cols] += picked_inverse(x1, map_leaf, leaf, i, place, sep1)


def downward(s_ref, k00, k01, k10, k11, chain, columns, constant, out, sigma, packed, *work):
    mid, upper = lax.axis_index("mid"), lax.axis_index("front") % 2
    order = sigma.shape[0]
    count = order // BLK
    for piece, m, u in ((k00, mid, upper), (k01, 1 - mid, upper),
                        (k10, mid, 1 - upper), (k11, 1 - mid, 1 - upper)):
        size = piece.shape[0]
        packed[pl.ds(pl.multiple_of((2 * m + u) * size, SUB), size), :] = piece[...]
    sigma[:, :order] = s_ref[...]
    sigma[:, order:] = columns[...]
    size = k00.shape[0]
    for m in range(count):
        pieces = [((m, m), 0, BLK, 0), (((m + 1) % count, m), BLK, BLK, 0)]
        if m < count // 2:
            pieces.append(((m + 2, m), 2 * BLK, BLK // 2, 0))
        else:
            pieces.append(((m, m - 2), 2 * BLK, BLK // 2, BLK // 2))
        for (i, j), start, rows, offset in pieces:
            value = packed[m * size + start:m * size + start + rows, :]
            first = i * BLK + offset
            sigma[first:first + rows, j * BLK:(j + 1) * BLK] -= value
            if i != j:
                sigma[j * BLK:(j + 1) * BLK, first:first + rows] -= value.T
    invert(sigma, work, solve=True)
    out[...] = dot(chain[...], sigma[:, order:]) + constant[...]


def square(order):
    return jax.ShapeDtypeStruct((order, order), jnp.float32)


def call(kernel, arrays, tables, outputs, scratch=(), cost=0, far=(), sems=()):
    vmem = pl.BlockSpec(memory_space=pltpu.VMEM)
    smem = pl.BlockSpec(memory_space=pltpu.SMEM)
    here = pl.BlockSpec(memory_space=pl.ANY)
    return pl.pallas_call(
        kernel,
        out_shape=outputs,
        in_specs=[vmem] * len(arrays) + [here] * len(far) + [smem] * len(tables),
        out_specs=jax.tree.map(lambda _: vmem, outputs),
        scratch_shapes=[pltpu.VMEM(s.shape, s.dtype) for s in scratch] + list(sems),
        compiler_params=pltpu.CompilerParams(vmem_limit_bytes=VMEM_BYTES),
        cost_estimate=pl.CostEstimate(flops=cost, bytes_accessed=cost, transcendentals=0),
    )(*arrays, *far, *tables)


def strip(rows):
    return jax.ShapeDtypeStruct((rows, BLK), jnp.float32)


def after(values, *others):
    return lax.optimization_barrier((values, others))[0]


def routes():
    fronts = lax.axis_size("front").bit_length() - 1
    members = lax.axis_size("member").bit_length() - 1
    return [("front", 1 << b) for b in range(1, fronts)] + [("member", 1 << b) for b in range(members)]


def crossing(pieces, number):
    steps = routes()
    return [swap(pieces[0], *steps[number]), swap(pieces[1], *steps[-1 - number])]


def cut(total):
    size = total.shape[0] // 2
    return [total[:size], total[size:]]


def add_pairs(pieces, got):
    return [pieces[0] + got[0], pieces[1] + got[1]]


def both_cores(pieces, got):
    own = [pieces[0], got[0], pieces[1], got[1]]
    return own + [swap(value, "front") for value in own]


def body(leaf_update, entries1, entries2, entries3, map_leaf, map_mid, map_top):
    low = map_mid.shape[1] * BLK
    sep1 = entries1.shape[0] * lax.axis_size("member") - low
    sep2 = entries2.shape[1] - map_top.shape[1] * BLK
    rest = map_top.shape[1] * BLK
    first = triangle(sep1 // BLK, 0) * BLK
    total = triangle((sep1 + low) // BLK, 0) * BLK
    halves = [strip(n // 2) for n in (first, first, total - first, total - first)]
    ss_keep, ss_send, rest_keep, rest_send = call(
        contribute, [leaf_update, entries1], [map_leaf], halves, [strip(total)]
    )
    last = len(routes()) - 1
    pieces = cut(ss_keep + swap(ss_send, "front"))
    for number in range(last):
        pieces = add_pairs(pieces, crossing(pieces, number))
    got = crossing(pieces, last)
    ss_parts = both_cores(pieces, got)
    rest_send = after(rest_send, pieces)
    pieces = cut(rest_keep + swap(rest_send, "front"))
    pieces = after(pieces, ss_parts[4:])
    got = crossing(pieces, 0)
    state = call(
        first_inverse, ss_parts, [], square(sep1), [strip(first)] + inverse_scratch(sep1), COST
    )
    for number in range(1, last + 1):
        pieces = add_pairs(pieces, after(got, state))
        got = crossing(pieces, number)
    other = [swap(value, "front") for value in pieces]
    state = after(state, other)
    x1 = call(first_inverse_end, [state], [], square(sep1), inverse_scratch(sep1), COST)
    got = after(got, x1)
    fetched = [swap(value, "front") for value in got]
    rest_parts = [pieces[0], got[0], pieces[1], got[1], other[0], fetched[0], other[1], fetched[1]]
    update = triangle(low // BLK, 0) * BLK
    rs, sent = call(
        first_update, [x1] + rest_parts, [],
        (jax.ShapeDtypeStruct((low, sep1), jnp.float32), strip(update // 2)),
        [strip(total - first)], COST,
    )
    got = swap(sent, "mid")
    shares = [sent, swap(sent, "front"), got, swap(got, "front")]
    schur = triangle(rest // BLK, 0) * BLK
    count = rest // BLK
    wide = jax.ShapeDtypeStruct((rest, rest + BLK), jnp.float32)
    dma = pltpu.SemaphoreType.DMA
    x2, t2, s, sent = call(
        second_level, shares, [map_mid, map_top],
        (square(sep2), jax.ShapeDtypeStruct((sep2, rest), jnp.float32), square(rest),
         strip(schur // 4)),
        [square(sep2 + rest), square(rest), wide, square(rest), strip(max(update, schur))]
        + inverse_scratch(sep2 + rest), 2 * COST,
        far=[entries2, entries3], sems=[dma, dma((count * (2 * count + 1),))],
    )
    got = swap(sent, "top")
    out = jax.ShapeDtypeStruct(leaf_update.shape, jnp.float32)
    columns = jax.ShapeDtypeStruct((rest, out.shape[1]), jnp.float32)
    chain, columns, constant = call(
        prepare, [x1, rs, x2, t2], [map_mid, map_leaf],
        (jax.ShapeDtypeStruct((low, rest), jnp.float32), columns, out),
        [jax.ShapeDtypeStruct((sep1, low), jnp.float32), square(low),
         jax.ShapeDtypeStruct((low, rest), jnp.float32), square(low)], COST // 2,
    )
    got = after(got, chain)
    pair = swap(got, "mid")
    pieces = [got, pair, swap(got, "front"), swap(pair, "front")]
    width = rest + out.shape[1]
    return call(
        downward, [s] + pieces + [chain, columns, constant], [], out,
        [jax.ShapeDtypeStruct((rest, width), jnp.float32), strip(schur)] + inverse_scratch(width),
        COST,
    )


def solution(mesh):
    leaves = mesh.shape["leaf"]
    fronts = mesh.shape["front"]
    grid = Mesh(mesh.devices.reshape(2, 2, leaves // 4, fronts), AXES)
    in_specs = (P(LEAF, "front"), P(LEAF, "front"), P(), P(), P(), P(), P())
    return jax.shard_map(
        body, mesh=grid, in_specs=in_specs, out_specs=P(LEAF, "front"), check_vma=False
    )
```

```python
import functools

import jax
import jax.numpy as jnp
from jax import lax
from jax.experimental import pallas as pl
from jax.experimental.pallas import tpu as pltpu
from jax.sharding import Mesh, PartitionSpec as P

BLK = 128
SUB = 8
AXES = ("top", "mid", "member", "front")
LEAF = AXES[:3]
VMEM_BYTES = 48 * 1024 * 1024
COST = 40_000_000


def swap(block, axis, distance=1):
    count = lax.axis_size(axis)
    return lax.ppermute(block, axis, [(i, i ^ distance) for i in range(count)])


def dot(left, right):
    return jnp.dot(left, right, precision=lax.Precision.HIGHEST, preferred_element_type=jnp.float32)


def dot_nt(left, right):
    dims = (((1,), (1,)), ((), ()))
    return lax.dot_general(
        left, right, dims, precision=lax.Precision.HIGHEST, preferred_element_type=jnp.float32
    )


def dot_tn(left, right):
    dims = (((0,), (0,)), ((), ()))
    return lax.dot_general(
        left, right, dims, precision=lax.Precision.HIGHEST, preferred_element_type=jnp.float32
    )


def block(index):
    return pl.ds(pl.multiple_of(index * BLK, BLK), BLK)


def column_of(panel, index):
    return jnp.broadcast_to(panel[:, index:index + 1], panel.shape)


def row_of(panel, index):
    return jnp.broadcast_to(panel[index:index + 1, :], panel.shape)


def minus_sum(value, terms):
    terms = list(terms)
    while len(terms) > 1:
        pairs = [terms[i] + terms[i + 1] for i in range(0, len(terms) - 1, 2)]
        terms = pairs + terms[2 * len(pairs):]
    return value - terms[0]


def eliminate_panel(columns, panel, ahead, row_id):
    columns, ahead = list(columns), list(ahead)
    pivot = row_of(columns[0], 0)
    for j in range(SUB):
        here = row_id == j
        scale = 1.0 / pivot
        factor = jnp.where(here, 0.0, columns[j]) * scale
        for m in range(j + 1, SUB):
            entry = row_of(columns[m], j)
            value = columns[m] - factor * entry
            if m == j + 1:
                pivot = row_of(value, m)
            columns[m] = jnp.where(here, entry * scale, value)
        for m in range(len(ahead)):
            entry = row_of(ahead[m], j)
            ahead[m] = jnp.where(here, entry * scale, ahead[m] - factor * entry)
        entry = row_of(panel, j)
        panel = jnp.where(here, entry * scale, panel - factor * entry)
    return panel, ahead


def eliminate_block(rows, between=()):
    rows = list(rows)
    count = len(rows)
    shape = rows[0].shape
    row_id = lax.broadcasted_iota(jnp.int32, shape, 0)
    lane_id = lax.broadcasted_iota(jnp.int32, shape, 1)
    slots = [(piece * (count - 4)) // max(len(between) - 1, 1) for piece in range(len(between))]
    before, scaled = [], []
    half = count // 2
    for start in (0, half):
        end = start + half
        left, right = [], []
        columns = [column_of(rows[start], SUB * start + j) for j in range(SUB)]
        for p in range(start, end):
            panel = rows[p]
            first, last = SUB * p, SUB * (p + 1)
            own = (lane_id >= first) & (lane_id < last)
            unit = (lane_id == first + row_id).astype(jnp.float32)
            before.append(jnp.where(lane_id < first, panel, unit))
            left.append(panel)
            ahead = []
            if p + 1 < end:
                ahead = [column_of(panel, last + j) for j in range(SUB)]
            panel, ahead = eliminate_panel(columns, jnp.where(own, unit, panel), ahead, row_id)
            scaled.append(jnp.where(lane_id < last, panel, 0.0))
            right.append(jnp.where((lane_id < last) | (lane_id >= SUB * end), panel, 0.0))
            if p + 1 < end:
                spread = [row_of(panel, k) for k in range(SUB)]
                near = [column_of(rows[p + 1], first + k) for k in range(SUB)]
                columns = [
                    minus_sum(
                        column_of(rows[p + 1], last + j),
                        [near[k] * row_of(ahead[j], k) for k in range(SUB)],
                    )
                    for j in range(SUB)
                ]
                for i in range(p + 1, end):
                    if i > p + 1:
                        near = [column_of(rows[i], first + k) for k in range(SUB)]
                    rows[i] = minus_sum(
                        jnp.where(own, 0.0, rows[i]), [near[k] * spread[k] for k in range(SUB)]
                    )
            for piece, slot in zip(between, slots):
                if slot == p:
                    piece()
        if end < count:
            change = dot_tn(jnp.concatenate(left, axis=0), jnp.concatenate(right, axis=0))
            inside = (lane_id >= SUB * start) & (lane_id < SUB * end)
            for i in range(end, count):
                rows[i] = jnp.where(inside, 0.0, rows[i]) - change[SUB * i:SUB * (i + 1), :]
    return jnp.concatenate(before, axis=0), jnp.concatenate(scaled, axis=0)


def inverse_scratch(width):
    return [strip(BLK)] * 4 + [jax.ShapeDtypeStruct((BLK, width), jnp.float32)]


def invert(ref, work, start=0, stop=None, solve=False, beside=()):
    pivot, before, scaled, inverse, spread = work
    order, width = ref.shape
    blocks = order // BLK
    stop = blocks if stop is None else stop

    def panels():
        return [pivot[SUB * i:SUB * (i + 1), :] for i in range(BLK // SUB)]

    def look_ahead(k, result):
        before[...], scaled[...] = result
        after_k = jnp.minimum(k + 1, blocks - 1)
        cross = ref[block(k), block(after_k)]
        change = dot_tn(dot(result[0], cross), dot(result[1], cross))
        pivot[...] = ref[block(after_k), block(after_k)] - change

    def update(k, first=0, last=width):
        here, cols = block(k), slice(first, last)
        shape = (BLK, last - first)
        lane_id = lax.broadcasted_iota(jnp.int32, shape, 1) + first
        row_id = lax.broadcasted_iota(jnp.int32, shape, 0)
        own = (lane_id >= k * BLK) & (lane_id < (k + 1) * BLK)

        def form():
            inverse[...] = dot_tn(before[...], scaled[...])

        def scale():
            unit = (lane_id - row_id == k * BLK).astype(jnp.float32)
            spread[:, cols] = dot(inverse[...], jnp.where(own, unit, ref[here, cols]))

        def change(i):
            rows = slice(i * BLK, (i + 1) * BLK)
            factor = jnp.where(k == i, 0.0, ref[rows, here])
            value = jnp.where(own, 0.0, ref[rows, cols]) - dot(factor, spread[:, cols])
            ref[rows, cols] = jnp.where(k == i, spread[:, cols], value)

        return [form, scale] + [functools.partial(change, i) for i in range(blocks)]

    def step(k, carry):
        look_ahead(k, eliminate_block(panels(), update(k - 1)))
        return carry

    pivot[...] = ref[block(start), block(start)]
    look_ahead(start, eliminate_block(panels(), beside))
    lax.fori_loop(start + 1, stop, step, 0)
    for piece in update(stop - 1, order if solve else 0):
        piece()
    return update(stop - 1, 0, order)[1:] if solve else []


def triangle(row, column):
    return row * (row + 1) // 2 + column


def lower_blocks(count):
    return [(i, j) for i in range(count) for j in range(i + 1)]


def packed_block(packed, index):
    return packed[pl.ds(pl.multiple_of(index * BLK, BLK), BLK), :]


def unpack(target, packed, first, count):
    for i, j in lower_blocks(count):
        value = packed_block(packed, first + triangle(i, j))
        rows, cols = slice(i * BLK, (i + 1) * BLK), slice(j * BLK, (j + 1) * BLK)
        target[rows, cols] = value
        if i != j:
            target[cols, rows] = value.T


def pack(target, full, count):
    for i, j in lower_blocks(count):
        place = triangle(i, j) * BLK
        target[place:place + BLK, :] = full[i * BLK:(i + 1) * BLK, j * BLK:(j + 1) * BLK]


def core_share(count, upper):
    assert count == 4
    a, b = 3 * upper, 1 + upper
    return [(a, a), ((a + 1) % 4, a), ((a + 2) % 4, a), (b, b), (b + 1, b)]


def add_blocks(target, packed, row_map, row):
    count = row_map.shape[1]
    for place, (i, j) in enumerate(core_share(count, 0) + core_share(count, 1)):
        a, b = block(row_map[row, i]), block(row_map[row, j])
        value = packed_block(packed, place)
        target[a, b] += value
        if i != j:
            target[b, a] += value.T


def selection(target, solved, row_map, row, sep):
    count = row_map.shape[1]
    shape = (BLK, target.shape[1])
    row_id = lax.broadcasted_iota(jnp.int32, shape, 0)
    lane_id = lax.broadcasted_iota(jnp.int32, shape, 1)
    for i in range(count):
        m = row_map[row, i]
        inside = m < sep
        source = solved[block(jnp.where(inside, m, 0)), :]
        unit = (lane_id - row_id == (m - sep) * BLK).astype(jnp.float32)
        target[i * BLK:(i + 1) * BLK, :] = jnp.where(inside, -source, unit)


def picked_inverse(inverse, row_map, row, i, j, sep):
    a, b = row_map[row, i], row_map[row, j]
    inside = (a < sep) & (b < sep)
    value = inverse[block(jnp.where(inside, a, 0)), block(jnp.where(inside, b, 0))]
    return jnp.where(inside, value, 0.0)


def node_index():
    return 2 * lax.axis_index("top") + lax.axis_index("mid")


def contribute(leaf_update, entries, map_leaf, ss_keep, ss_send, rest_keep, rest_send, packed):
    members = lax.axis_size("member")
    member = lax.axis_index("member")
    column = lax.axis_index("front")
    upper = column % 2
    leaf = node_index() * members + member
    packed[...] = jnp.zeros(packed.shape, packed.dtype)
    rows, width = entries.shape
    height = min(rows, BLK)
    for i in range(rows // height):
        start = member * rows + i * height
        r = start // BLK
        for j in range(width // BLK):
            c = column * (width // BLK) + j

            @pl.when(r >= c)
            def _():
                place = pl.multiple_of(triangle(r, c) * BLK + start % BLK, height)
                packed[pl.ds(place, height), :] = (
                    entries[i * height:(i + 1) * height, j * BLK:(j + 1) * BLK]
                )

    width = leaf_update.shape[1] // BLK
    for j in range(width):
        c = map_leaf[leaf, column * width + j]
        for i in range(map_leaf.shape[1]):
            r = map_leaf[leaf, i]

            @pl.when(r >= c)
            def _():
                place = block(triangle(r, c))
                packed[place, :] += leaf_update[i * BLK:(i + 1) * BLK, j * BLK:(j + 1) * BLK]

    first = 2 * ss_keep.shape[0]
    for keep, send, start in ((ss_keep, ss_send, 0), (rest_keep, rest_send, first)):
        half = keep.shape[0]
        keep[...] = packed[pl.ds(pl.multiple_of(start + upper * half, SUB), half), :]
        send[...] = packed[pl.ds(pl.multiple_of(start + (1 - upper) * half, SUB), half), :]


def join(target, parts, upper):
    size = parts[0].shape[0]
    for p in range(4):
        side = upper if p < 2 else 1 - upper
        start = pl.multiple_of((2 * side + p % 2) * size, SUB)
        target[pl.ds(start, size), :] = parts[2 * p][...] + parts[2 * p + 1][...]


def first_inverse(*refs):
    parts, (x_ref, packed, *work) = refs[:8], refs[8:]
    join(packed, parts, lax.axis_index("front") % 2)
    blocks = x_ref.shape[0] // BLK
    unpack(x_ref, packed, 0, blocks)
    invert(x_ref, work, 0, blocks // 2)


def first_inverse_end(half_ref, x_ref, *work):
    x_ref[...] = half_ref[...]
    blocks = x_ref.shape[0] // BLK
    invert(x_ref, work, blocks // 2, blocks)


def first_update(*refs):
    x_ref, parts, (rs, send, packed) = refs[0], refs[1:9], refs[9:]
    upper = lax.axis_index("front") % 2
    join(packed, parts, upper)
    sep, low = x_ref.shape[0] // BLK, rs.shape[0] // BLK
    first = triangle(sep, 0)
    for i in range(low):
        for j in range(sep):
            rs[i * BLK:(i + 1) * BLK, j * BLK:(j + 1) * BLK] = packed_block(
                packed, triangle(sep + i, j) - first
            )
    for side in range(2):

        @pl.when(upper == side)
        def _():
            share = core_share(low, side)
            columns = sorted({j for _, j in share})
            rows = jnp.concatenate([rs[j * BLK:(j + 1) * BLK, :] for j in columns], axis=0)
            solved = dot_nt(x_ref[...], rows)
            for place, (i, j) in enumerate(share):
                number = triangle(sep + max(i, j), sep + min(i, j)) - first
                value = packed_block(packed, number)
                value = value if i >= j else value.T
                at = columns.index(j) * BLK
                change = dot(rs[i * BLK:(i + 1) * BLK, :], solved[:, at:at + BLK])
                send[place * BLK:(place + 1) * BLK, :] = value - change


def second_level(mine, pair, got, got_pair, entries, top, map_mid, map_top, x_ref, t_ref, s_ref,
                 send, front, cross, low, own_top, packed, *rest):
    *work, front_sem, sems = rest
    sep, order = x_ref.shape[0], front.shape[0]
    count = map_top.shape[1]
    node = lax.axis_index("top")
    mid = lax.axis_index("mid")
    upper = lax.axis_index("front") % 2
    child = node_index()
    part = 2 * mid + upper
    start = pl.multiple_of(node * order, BLK)
    front_copy = pltpu.make_async_copy(entries.at[pl.ds(start, order), :], front, front_sem)
    front_copy.start()
    copies = []

    def fetch(row, column, target, i, j):
        place = target.at[i * BLK:(i + 1) * BLK, j * BLK:(j + 1) * BLK]
        copy = pltpu.make_async_copy(top.at[block(row), block(column)], place, sems.at[len(copies)])
        copy.start()
        copies.append(copy)

    for i in range(count):
        for j in range(count):
            fetch(map_top[node, i], map_top[node, j], own_top, i, j)
            fetch(map_top[1 - node, i], map_top[node, j], cross, i, j)
        fetch(map_top[node, i], map_top[1 - node, part], low, i, count)
    front_copy.wait()
    half = got.shape[0]
    for own, other, source in ((mine, pair, child), (got, got_pair, child + 1 - 2 * mid)):
        packed[pl.ds(pl.multiple_of(upper * half, SUB), half), :] = own[...]
        packed[pl.ds(pl.multiple_of((1 - upper) * half, SUB), half), :] = other[...]
        add_blocks(front, packed, map_mid, source)
    later = invert(front.at[:sep, :], work, solve=True)
    t_ref[...] = front[:sep, sep:]
    for copy in copies:
        copy.wait()

    def update(i):
        rows = slice(i * BLK, (i + 1) * BLK)
        below = slice(sep + i * BLK, sep + (i + 1) * BLK)
        value = front[below, sep:] - dot(front[below, :sep], t_ref[...]) + own_top[rows, :]
        s_ref[rows, :] = value
        low[rows, :count * BLK] = value

    update(0)
    later += [functools.partial(update, i) for i in range(1, count)]
    invert(low, work, solve=True, beside=later)
    x_ref[...] = front[:sep, :sep]
    solved = low[:, count * BLK:]
    send[:BLK, :] = dot(cross[block(part), :], solved)
    send[BLK:2 * BLK, :] = dot(cross[block((part + 1) % count), :], solved)
    far = dot(cross[block((part + 2) % count), :], solved)
    start = jnp.where(part < count // 2, 0, BLK // 2)
    packed[:BLK, :] = jnp.where(part < count // 2, far, far.T)
    send[2 * BLK:, :] = packed[pl.ds(pl.multiple_of(start, SUB), BLK // 2), :]


def prepare(x1, rs, x2, t2, map_mid, map_leaf, chain, columns, constant, t1, near, far, picked):
    sep2, sep1 = x2.shape[0] // BLK, x1.shape[0] // BLK
    child = node_index()
    leaf = child * lax.axis_size("member") + lax.axis_index("member")
    column = lax.axis_index("front")
    t1[...] = dot_nt(x1[...], rs[...])
    selection(near, t1, map_leaf, leaf, sep1)
    selection(far, t2, map_mid, child, sep2)
    chain[...] = dot(near[...], far[...])
    count = map_mid.shape[1]
    for i in range(count):
        for j in range(count):
            rows, cols = slice(i * BLK, (i + 1) * BLK), slice(j * BLK, (j + 1) * BLK)
            picked[rows, cols] = picked_inverse(x2, map_mid, child, i, j, sep2)
    width = constant.shape[1]
    columns[...] = chain[pl.ds(pl.multiple_of(column * width, BLK), width), :].T
    mine = near[pl.ds(pl.multiple_of(column * width, BLK), width), :]
    constant[...] = dot(near[...], dot_nt(picked[...], mine))
    for i in range(map_leaf.shape[1]):
        for j in range(width // BLK):
            rows, cols = slice(i * BLK, (i + 1) * BLK), slice(j * BLK, (j + 1) * BLK)
            place = column * (width // BLK) + j
            constant[rows, cols] += picked_inverse(x1, map_leaf, leaf, i, place, sep1)


def downward(s_ref, k00, k01, k10, k11, chain, columns, constant, out, sigma, packed, *work):
    mid, upper = lax.axis_index("mid"), lax.axis_index("front") % 2
    order = sigma.shape[0]
    count = order // BLK
    for piece, m, u in ((k00, mid, upper), (k01, 1 - mid, upper),
                        (k10, mid, 1 - upper), (k11, 1 - mid, 1 - upper)):
        size = piece.shape[0]
        packed[pl.ds(pl.multiple_of((2 * m + u) * size, SUB), size), :] = piece[...]
    sigma[:, :order] = s_ref[...]
    sigma[:, order:] = columns[...]
    size = k00.shape[0]
    for m in range(count):
        pieces = [((m, m), 0, BLK, 0), (((m + 1) % count, m), BLK, BLK, 0)]
        if m < count // 2:
            pieces.append(((m + 2, m), 2 * BLK, BLK // 2, 0))
        else:
            pieces.append(((m, m - 2), 2 * BLK, BLK // 2, BLK // 2))
        for (i, j), start, rows, offset in pieces:
            value = packed[m * size + start:m * size + start + rows, :]
            first = i * BLK + offset
            sigma[first:first + rows, j * BLK:(j + 1) * BLK] -= value
            if i != j:
                sigma[j * BLK:(j + 1) * BLK, first:first + rows] -= value.T
    invert(sigma, work, solve=True)
    out[...] = dot(chain[...], sigma[:, order:]) + constant[...]


def square(order):
    return jax.ShapeDtypeStruct((order, order), jnp.float32)


def call(kernel, arrays, tables, outputs, scratch=(), cost=0, far=(), sems=()):
    vmem = pl.BlockSpec(memory_space=pltpu.VMEM)
    smem = pl.BlockSpec(memory_space=pltpu.SMEM)
    here = pl.BlockSpec(memory_space=pl.ANY)
    return pl.pallas_call(
        kernel,
        out_shape=outputs,
        in_specs=[vmem] * len(arrays) + [here] * len(far) + [smem] * len(tables),
        out_specs=jax.tree.map(lambda _: vmem, outputs),
        scratch_shapes=[pltpu.VMEM(s.shape, s.dtype) for s in scratch] + list(sems),
        compiler_params=pltpu.CompilerParams(vmem_limit_bytes=VMEM_BYTES),
        cost_estimate=pl.CostEstimate(flops=cost, bytes_accessed=cost, transcendentals=0),
    )(*arrays, *far, *tables)


def strip(rows):
    return jax.ShapeDtypeStruct((rows, BLK), jnp.float32)


def after(values, *others):
    return lax.optimization_barrier((values, others))[0]


def routes():
    fronts = lax.axis_size("front").bit_length() - 1
    members = lax.axis_size("member").bit_length() - 1
    return [("front", 1 << b) for b in range(1, fronts)] + [("member", 1 << b) for b in range(members)]


def crossing(pieces, number):
    steps = routes()
    return [swap(pieces[0], *steps[number]), swap(pieces[1], *steps[-1 - number])]


def cut(total):
    size = total.shape[0] // 2
    return [total[:size], total[size:]]


def add_pairs(pieces, got):
    return [pieces[0] + got[0], pieces[1] + got[1]]


def both_cores(pieces, got):
    own = [pieces[0], got[0], pieces[1], got[1]]
    return own + [swap(value, "front") for value in own]


def body(leaf_update, entries1, entries2, entries3, map_leaf, map_mid, map_top):
    low = map_mid.shape[1] * BLK
    sep1 = entries1.shape[0] * lax.axis_size("member") - low
    sep2 = entries2.shape[1] - map_top.shape[1] * BLK
    rest = map_top.shape[1] * BLK
    first = triangle(sep1 // BLK, 0) * BLK
    total = triangle((sep1 + low) // BLK, 0) * BLK
    halves = [strip(n // 2) for n in (first, first, total - first, total - first)]
    ss_keep, ss_send, rest_keep, rest_send = call(
        contribute, [leaf_update, entries1], [map_leaf], halves, [strip(total)]
    )
    last = len(routes()) - 1
    pieces = cut(ss_keep + swap(ss_send, "front"))
    for number in range(last):
        pieces = add_pairs(pieces, crossing(pieces, number))
    got = crossing(pieces, last)
    ss_parts = both_cores(pieces, got)
    rest_send = after(rest_send, pieces)
    pieces = cut(rest_keep + swap(rest_send, "front"))
    pieces = after(pieces, ss_parts[4:])
    got = crossing(pieces, 0)
    state = call(
        first_inverse, ss_parts, [], square(sep1), [strip(first)] + inverse_scratch(sep1), COST
    )
    for number in range(1, last + 1):
        pieces = add_pairs(pieces, after(got, state))
        got = crossing(pieces, number)
    other = [swap(value, "front") for value in pieces]
    state = after(state, other)
    x1 = call(first_inverse_end, [state], [], square(sep1), inverse_scratch(sep1), COST)
    got = after(got, x1)
    fetched = [swap(value, "front") for value in got]
    rest_parts = [pieces[0], got[0], pieces[1], got[1], other[0], fetched[0], other[1], fetched[1]]
    update = triangle(low // BLK, 0) * BLK
    rs, sent = call(
        first_update, [x1] + rest_parts, [],
        (jax.ShapeDtypeStruct((low, sep1), jnp.float32), strip(update // 2)),
        [strip(total - first)], COST,
    )
    got = swap(sent, "mid")
    shares = [sent, swap(sent, "front"), got, swap(got, "front")]
    schur = triangle(rest // BLK, 0) * BLK
    count = rest // BLK
    wide = jax.ShapeDtypeStruct((rest, rest + BLK), jnp.float32)
    dma = pltpu.SemaphoreType.DMA
    x2, t2, s, sent = call(
        second_level, shares, [map_mid, map_top],
        (square(sep2), jax.ShapeDtypeStruct((sep2, rest), jnp.float32), square(rest),
         strip(schur // 4)),
        [square(sep2 + rest), square(rest), wide, square(rest), strip(max(update, schur))]
        + inverse_scratch(sep2 + rest), 2 * COST,
        far=[entries2, entries3], sems=[dma, dma((count * (2 * count + 1),))],
    )
    got = swap(sent, "top")
    out = jax.ShapeDtypeStruct(leaf_update.shape, jnp.float32)
    columns = jax.ShapeDtypeStruct((rest, out.shape[1]), jnp.float32)
    chain, columns, constant = call(
        prepare, [x1, rs, x2, t2], [map_mid, map_leaf],
        (jax.ShapeDtypeStruct((low, rest), jnp.float32), columns, out),
        [jax.ShapeDtypeStruct((sep1, low), jnp.float32), square(low),
         jax.ShapeDtypeStruct((low, rest), jnp.float32), square(low)], COST // 2,
    )
    got = after(got, chain)
    pair = swap(got, "mid")
    pieces = [got, pair, swap(got, "front"), swap(pair, "front")]
    width = rest + out.shape[1]
    return call(
        downward, [s] + pieces + [chain, columns, constant], [], out,
        [jax.ShapeDtypeStruct((rest, width), jnp.float32), strip(schur)] + inverse_scratch(width),
        COST,
    )


def solution(mesh):
    leaves = mesh.shape["leaf"]
    fronts = mesh.shape["front"]
    grid = Mesh(mesh.devices.reshape(2, 2, leaves // 4, fronts), AXES)
    in_specs = (P(LEAF, "front"), P(LEAF, "front"), P(), P(), P(), P(), P())
    return jax.shard_map(
        body, mesh=grid, in_specs=in_specs, out_specs=P(LEAF, "front"), check_vma=False
    )
```
